512 devices in a mesh: dp: 32 (over z, core), tensor: 16 (over x, y).
Axes of the slice: x: 4, y: 4, z: 16, core: 2. Of those that a mesh axis runs over, the one named last changes fastest.
Arguments:
- resid: bfloat16 [4096, 8192], P('dp', 'tensor'), may hold values from -6 to 6
- context: bfloat16 [4096, 4096], P('dp', 'tensor'), may hold values from -6 to 6
- out_weight: bfloat16 [4096, 8192], P('tensor', 'dp'), may hold values from -0.1875 to 0.1875
- owners: int32 [4096, 1], P('dp'), may hold values from 0 to 31; in each aligned block of 128 rows (0 to 127, 128 to 255, ...) at most 8 rows name the same one
- query_lengths: int32 [32], replicated, may hold values from 96 to 128, as said below
- student_rows: bfloat16 [4096, 2048], P('dp'), may hold values from -6 to 6
- up_weight: bfloat16 [2048, 2816], P(None, 'tensor'), may hold values from -0.125 to 0.125
- down_weight: bfloat16 [2048, 2816], P(None, 'tensor'), may hold values from -0.109375 to 0.109375
- proj_weight: bfloat16 [2048, 8192], P(None, 'tensor'), may hold values from -0.125 to 0.125
Outputs:
- owner_loss: float32 [32], P('dp')
- grad_up: float32 [2048, 2816], P('dp', 'tensor')
- grad_down: float32 [2048, 2816], P('dp', 'tensor')
The draws below stay inside these ranges and needn't reach their ends.
Inputs may be any that keep to these rules, and one draw needn't show every extreme that they name: `owners`: among the rows of one index of dp no owner is named more than 8 times, a bound that some block reaches. `query_lengths`: some index of dp has all 128 rows live.
All inputs are finite; a program needn't handle non-finite values.
Results may differ from the reference program's by a relative error of at most 0.0075.
Values may be sent and summed in bfloat16 or wider, within the bound.
No kernel may reach another device: no remote copies, remote signals or barrier semaphores. Data moves between devices by JAX's collectives and lax.ppermute only.
A program may use at most 64 MiB of HBM per device.

```python
import math
import jax
import jax.numpy as jnp
import numpy as np
from jax import lax

D = 8192
CTXW = 4096
DS = 2048
FFS = 2816
QROWS = 128
CAP = 8
SLOTS = 256
QTOK = 4096
N_DP = 32
N_TENSOR = 16


def draw_query_lengths(key, part):
    key = jax.random.fold_in(key, 7)
    first, second = jax.random.split(key)
    lengths = jax.random.randint(first, (N_DP,), 3 * QROWS // 4, QROWS + 1)
    fullest = jax.random.randint(second, (), 0, N_DP)
    return jnp.where(jnp.arange(N_DP) == fullest, QROWS, lengths).astype(jnp.int32)


def raised(result, stream_key, source, target, parts, factor):
    def block_of(axis_at):
        return (jnp.arange(result.shape[axis_at]) // (result.shape[axis_at] // parts)).reshape((-1,) + (1,) * (result.ndim - 1 - axis_at))

    near = jax.random.permutation(stream_key, parts)[block_of(target)]
    second = (block_of(target) + parts // 2) % parts
    return jnp.where((block_of(source) == near) | (block_of(source) == second), factor * result, result)


def block_levels(stream_key, dims, cuts, smallest, largest):
    loudness = 1.0
    for axis_at, parts in cuts:
        draws = jax.random.uniform(jax.random.fold_in(jax.random.fold_in(stream_key, 6), axis_at), (parts,), jnp.float32, smallest / len(cuts), largest / len(cuts))
        loudness = loudness * jnp.repeat(jnp.exp(draws), dims[axis_at] // parts).reshape((-1,) + (1,) * (len(dims) - 1 - axis_at))
    return loudness


def shared_out(own_key, own, number, rows, number_of, top, bound, lean):
    order = jax.random.permutation(own_key, number_of)
    packed, ordinary = shares(number_of, rows * top, bound, lean, True), shares(number_of, rows * top, bound, lean, False)
    places = jnp.arange(number_of)

    def named(sizes, offset_by):
        used = int((sizes > 0).sum())
        fixed = max(1, used // 4)
        moved = fixed + (places - fixed + offset_by * (used - fixed)) % max(1, number_of - fixed)
        return jnp.zeros((number_of,), jnp.int32).at[order[jnp.where(places < fixed, places, moved)]].set(jnp.asarray(sizes, jnp.int32))

    sizes = jnp.where(number % 4 == 0, named(packed, number // 4), named(ordinary, number - number // 4 - 1))
    mixed = jax.random.permutation(jax.random.fold_in(own, 3), number_of)
    source_of, receiver = mixed[0:number_of // 2 * 2:2], mixed[1:number_of // 2 * 2:2]
    margin = jnp.minimum(sizes[source_of] - 1, bound - sizes[receiver]) // 2
    margin = jnp.where((source_of == order[0]) | (receiver == order[0]) | (sizes[receiver] == 0), 0, jnp.maximum(margin, 0))
    moved = jax.random.randint(jax.random.fold_in(own, 4), (number_of // 2,), 0, 1 << 20) % (margin + 1)
    sizes = sizes.at[source_of].add(-moved).at[receiver].add(moved)
    items = jnp.searchsorted(jnp.cumsum(sizes), jnp.arange(rows * top), side="right").astype(jnp.int32)
    table = items.reshape(top, rows).T
    table = table[jax.random.permutation(jax.random.fold_in(own, 1), rows)]
    offset_by = jax.random.randint(jax.random.fold_in(own, 2), (rows, 1), 0, top)
    return jnp.take_along_axis(table, (jnp.arange(top)[None, :] + offset_by) % top, axis=1)


def shares(amount, total, bound, skew, full):
    weights = [(1 << 20) // math.isqrt(grade ** skew) + 1 for grade in range(1, amount + 1)]
    largest = bound if full else min(bound, max(-(-total // amount), total * weights[0] // sum(weights)))
    least = 1 if total - largest >= amount - 1 else 0
    holding, spare = [largest] + [least] * (amount - 1), total - largest - least * (amount - 1)
    while spare > 0:
        movable = [i for i in range(1, amount) if holding[i] < largest] or [i for i in range(1, amount) if holding[i] < bound]
        mass, left = sum([weights[i] for i in movable]), spare
        for i in movable:
            extra = min(bound - holding[i], max(1, left * weights[i] // mass), spare)
            holding[i] = holding[i] + extra
            spare = spare - extra
    return np.array(holding)


def centred(stream_key, shape, scale, most, cuts=(), held_as=jnp.bfloat16):
    factor_of = block_levels(stream_key, shape, cuts, -0.22, 0.18) if cuts else 1.0
    values = jax.random.normal(stream_key, shape, jnp.float32) * scale * factor_of
    return jnp.minimum(jnp.maximum(values, -most), most).astype(held_as)


def gaussian_with(own_key, dims, deviation, limit, shards, heavy, held_as=jnp.bfloat16):
    entries = deviation * jax.random.normal(own_key, dims, jnp.float32)
    if shards:
        entries = entries * block_levels(own_key, dims, shards, -0.22, 0.18)
    return jnp.clip(raised(entries, jax.random.fold_in(own_key, 3), *heavy), -limit, limit).astype(held_as)


def setup_inputs(seed: int = 0) -> dict:
    seeds = jax.random.split(jax.random.key(seed), 10)
    resid = centred(seeds[0], (QTOK, D), 1.0, 6.0, ((0, 32), (1, 16)))
    context = centred(seeds[1], (QTOK, CTXW), 1.0, 6.0, ((0, 32), (1, 16)))
    out_weight = gaussian_with(seeds[2], (CTXW, D), CTXW ** -0.5, 0.1875, ((0, 16), (1, 32)), (0, 1, 32, 2.75))
    owners_keys = jax.random.split(jax.random.fold_in(seeds[3], 1), QTOK // QROWS)
    owners_turns = jax.random.permutation(jax.random.fold_in(seeds[3], 3), QTOK // QROWS)
    owners = jax.vmap(lambda own, number: shared_out(jax.random.fold_in(seeds[3], 2), own, number, QROWS, N_DP, 1, CAP, 2))(owners_keys, owners_turns).reshape((QTOK, 1))
    query_lengths = draw_query_lengths(jax.random.fold_in(seeds[9], 71), 0)
    student_rows = centred(seeds[5], (QTOK, DS), 1.0, 6.0, ((0, 32),))
    up_weight = centred(seeds[6], (DS, FFS), DS ** -0.5, 0.125, ((1, 16),))
    down_weight = centred(seeds[7], (DS, FFS), FFS ** -0.5, 0.109375, ((1, 16),))
    proj_weight = centred(seeds[8], (DS, D), DS ** -0.5, 0.125, ((1, 16),))
    return dict(resid=resid, context=context, out_weight=out_weight, owners=owners, query_lengths=query_lengths, student_rows=student_rows, up_weight=up_weight, down_weight=down_weight, proj_weight=proj_weight)


def student_pass(student_in, target_rows, live_rows, loss_scale, up_weight, down_weight, proj_weight):
    inputs = student_in.astype(jnp.float32)
    normed = (inputs * lax.rsqrt(lax.optimization_barrier(jnp.mean(inputs * inputs, axis=-1, keepdims=True)) + 1e-05)).astype(jnp.bfloat16)
    preact = jnp.dot(normed, up_weight, preferred_element_type=jnp.float32)
    hidden = jax.nn.silu(preact).astype(jnp.bfloat16)
    mixed = lax.dot_general(hidden, down_weight, (((1,), (1,)), ((), ())), preferred_element_type=jnp.float32)
    updated = (inputs + mixed).astype(jnp.bfloat16)
    projected = jnp.dot(updated, proj_weight, preferred_element_type=jnp.float32)
    residue = projected - target_rows.astype(jnp.float32)
    squares = jnp.sum(live_rows * lax.optimization_barrier(jnp.sum(residue * residue, axis=-1)))
    cotangent = (2.0 * loss_scale * live_rows[:, None] * residue).astype(jnp.bfloat16)
    back_sum = lax.dot_general(cotangent, proj_weight, (((1,), (1,)), ((), ())), preferred_element_type=jnp.float32)
    out_grad = back_sum.astype(jnp.bfloat16)
    grad_down = lax.dot_general(out_grad, hidden, (((0,), (0,)), ((), ())), preferred_element_type=jnp.float32)
    hidden_grad = jnp.dot(out_grad, down_weight, preferred_element_type=jnp.float32)
    gate_sig = jax.nn.sigmoid(preact)
    pre_grad = (hidden_grad * gate_sig * (1.0 + preact * (1.0 - gate_sig))).astype(jnp.bfloat16)
    grad_up = lax.dot_general(normed, pre_grad, (((0,), (0,)), ((), ())), preferred_element_type=jnp.float32)
    return (squares * loss_scale, grad_up, grad_down)

def reference(resid, context, out_weight, owners, query_lengths, student_rows, up_weight, down_weight, proj_weight):
    block = CTXW // N_TENSOR
    summed = jnp.zeros((QTOK, D), jnp.float32)
    for number in range(N_TENSOR):
        partial_value = jnp.dot(context[:, number * block:(number + 1) * block], out_weight[number * block:(number + 1) * block], preferred_element_type=jnp.float32)
        summed = summed + lax.optimization_barrier(partial_value.astype(jnp.bfloat16)).astype(jnp.float32)
    target = (resid.astype(jnp.float32) + summed).astype(jnp.bfloat16)
    owner_map = owners[:, 0].reshape(N_DP, QROWS)
    position = jnp.arange(QROWS, dtype=jnp.int32)
    valid = position[None, :] < query_lengths[:, None]
    same = (owner_map[:, :, None] == owner_map[:, None, :]) & valid[:, None, :] & (position[None, None, :] < position[None, :, None])
    rank_index = lax.optimization_barrier(jnp.sum(same.astype(jnp.int32), axis=2))
    source = jnp.arange(N_DP, dtype=jnp.int32)[:, None]
    slot_index = source * CAP + rank_index
    row_index = source * QROWS + position[None, :]
    table = jnp.full((N_DP, SLOTS), QTOK, jnp.int32)
    table = table.at[jnp.where(valid, owner_map, N_DP).astype(jnp.int32), jnp.where(valid, slot_index, 0).astype(jnp.int32)].set(row_index.astype(jnp.int32), mode='drop')
    target_pad = jnp.concatenate([target, jnp.zeros((1, D), jnp.bfloat16)], axis=0)
    student_pad = jnp.concatenate([student_rows, jnp.zeros((1, DS), jnp.bfloat16)], axis=0)
    total_live = jnp.sum(query_lengths).astype(jnp.float32)
    loss_scale = N_DP / (total_live * D)

    def owner_step(carry, index_row):
        live_rows = (index_row < QTOK).astype(jnp.float32)
        loss, grad_up, grad_down = student_pass(student_pad[index_row], target_pad[index_row], live_rows, loss_scale, up_weight, down_weight, proj_weight)
        return ((carry[0] + grad_up, carry[1] + grad_down), loss)
    start = (jnp.zeros((DS, FFS), jnp.float32), jnp.zeros((DS, FFS), jnp.float32))
    grads, owner_loss = lax.scan(owner_step, start, table)
    return (owner_loss, grads[0], grads[1])
```

```python
import jax
import jax.numpy as jnp
from jax import lax
from jax.sharding import PartitionSpec as P

D = 8192
F32 = jnp.float32
BF16 = jnp.bfloat16

CORES = [(d, d ^ 1) for d in range(32)]
NEAR = [[8 * h + 2 * l + c for l in range(4)] for h in range(4) for c in range(2)]
FAR = [[8 * h + 2 * l + c for h in range(4)] for l in range(4) for c in range(2)]


def flat(zh, zl, c, x, y):
    return (8 * zh + 2 * zl + c) * 16 + 4 * x + y


HOME = [
    (flat(zh, zl, c, x, y), flat(x, zl, c, zh, y))
    for zh in range(4)
    for zl in range(4)
    for c in range(2)
    for x in range(4)
    for y in range(4)
]


def swap_all(x, axis, groups=None):
    return lax.all_to_all(x, axis, split_axis=0, concat_axis=0, tiled=True, axis_index_groups=groups)


def spread(x, axis, count, groups=None):
    return swap_all(jnp.broadcast_to(x[None], (count,) + x.shape), axis, groups)


def sum_rows(part, beside=None):
    rows, width = part.shape
    pieces = part.astype(BF16).reshape(16, rows // 16, width)
    if beside is not None:
        beside = jnp.broadcast_to(beside[None, None, :], (16, rows // 16, beside.shape[0]))
        pieces = jnp.concatenate([pieces, beside], axis=2)
    return jnp.sum(swap_all(pieces, "tensor").astype(F32), axis=0)


def halves(x):
    high = lax.reduce_precision(x, 8, 7)
    return high.astype(BF16), (x - high).astype(BF16)


def packed(terms, loss):
    high, low = (part[..., None, None] for part in halves(loss))
    lane = jnp.arange(32, dtype=jnp.int32)
    side = jnp.where(lane == 0, high, jnp.where(lane == 1, low, jnp.zeros((), BF16)))
    side = jnp.broadcast_to(side, terms.shape[:-1] + (32,))
    return jnp.concatenate([terms.astype(BF16), side], axis=-1)


def unpacked(x):
    return x[..., :352], x[..., 0, 352] + x[..., 0, 353]


def all_rows(x):
    return spread(x, "tensor", 16).reshape(16 * x.shape[0], x.shape[1])


def on_device(
    resid,
    context,
    out_weight,
    owners,
    query_lengths,
    student_rows,
    up_weight,
    down_weight,
    proj_weight,
):
    dp = lax.axis_index("dp")
    tensor = lax.axis_index("tensor")
    core = dp % 2
    rows4 = lax.all_gather(context, "dp", axis_index_groups=FAR).reshape(512, 256)
    cols4 = lax.all_gather(out_weight, "dp", axis_index_groups=NEAR)
    cols4_other = lax.ppermute(cols4, "dp", CORES)
    first = jnp.where(core == 0, cols4, cols4_other)
    second = jnp.where(core == 0, cols4_other, cols4)
    wide = jnp.stack([first, second], axis=2)
    head = lax.dot_general(rows4, wide, (((1,), (1,)), ((), ())), preferred_element_type=F32)
    head = head.astype(BF16).reshape(4, 128, 4, 512).transpose(0, 2, 1, 3).reshape(16, 128, 512)
    head_sum = jnp.sum(swap_all(head, "tensor").astype(F32), axis=0).astype(BF16)
    head_sum = lax.ppermute(head_sum, ("dp", "tensor"), HOME)
    target = (resid.astype(F32) + head_sum.astype(F32)).astype(BF16)

    inputs = student_rows.astype(F32)
    normed = (inputs * lax.rsqrt(jnp.mean(inputs * inputs, axis=-1, keepdims=True) + 1e-05)).astype(
        BF16
    )
    preact = jnp.dot(normed, up_weight, preferred_element_type=F32)
    hidden = jax.nn.silu(preact).astype(BF16)
    mixed_part = lax.dot_general(
        hidden, down_weight, (((1,), (1,)), ((), ())), preferred_element_type=F32
    )
    own_inputs = lax.dynamic_slice_in_dim(student_rows, tensor * 8, 8, axis=0).astype(F32)
    updated = all_rows((own_inputs + sum_rows(mixed_part)).astype(BF16))
    projected = jnp.dot(updated, proj_weight, preferred_element_type=F32)

    total_live = jnp.sum(query_lengths).astype(F32)
    loss_scale = 32.0 / (total_live * D)
    own_length = lax.dynamic_index_in_dim(query_lengths, dp, keepdims=False)
    live = (jnp.arange(128, dtype=jnp.int32) < own_length).astype(F32)
    residue = projected - target.astype(F32)
    squares = live * jnp.sum(residue * residue, axis=-1)
    named = (owners == jnp.arange(32, dtype=jnp.int32)[None, :]).astype(F32)
    loss_part = jnp.sum(named * squares[:, None], axis=0)

    cotangent = (2.0 * loss_scale * live[:, None] * residue).astype(BF16)
    back_part = lax.dot_general(
        cotangent, proj_weight, (((1,), (1,)), ((), ())), preferred_element_type=F32
    )
    side = jnp.concatenate(halves(loss_part) + (jnp.zeros((64,), BF16),))
    back_sum = sum_rows(back_part, side)
    out_grad = all_rows(back_sum[:, :2048].astype(BF16))
    losses = back_sum[0, 2048:2080] + back_sum[0, 2080:2112]
    hidden_grad = jnp.dot(out_grad, down_weight, preferred_element_type=F32)
    gate_sig = jax.nn.sigmoid(preact)
    pre_grad = (hidden_grad * gate_sig * (1.0 + preact * (1.0 - gate_sig))).astype(BF16)
    down_term = lax.dot_general(
        out_grad, hidden, (((0,), (0,)), ((), ())), preferred_element_type=F32
    )
    up_term = lax.dot_general(
        normed, pre_grad, (((0,), (0,)), ((), ())), preferred_element_type=F32
    )
    terms = jnp.concatenate([up_term, down_term], axis=1).astype(BF16)
    terms = terms.reshape(4, 4, 2, 64, 352)
    losses = losses.reshape(4, 4, 2)
    mine, other = (
        packed(
            jnp.where(core == which, terms[:, :, 0], terms[:, :, 1]),
            jnp.where(core == which, losses[:, :, 0], losses[:, :, 1]),
        )
        for which in (0, 1)
    )
    pair = mine.astype(F32) + lax.ppermute(other, "dp", CORES).astype(F32)
    pair = packed(*unpacked(pair)).transpose(1, 0, 2, 3)
    near = jnp.sum(swap_all(pair, "dp", NEAR).astype(F32), axis=0)
    total = jnp.sum(swap_all(packed(*unpacked(near)), "dp", FAR).astype(F32), axis=0)
    total, loss = unpacked(total)
    return (jnp.reshape(loss * loss_scale, (1,)), total[:, :176], total[:, 176:])


def solution(mesh):
    return jax.shard_map(
        on_device,
        mesh=mesh,
        in_specs=(
            P("dp", "tensor"),
            P("dp", "tensor"),
            P("tensor", "dp"),
            P("dp", None),
            P(),
            P("dp", None),
            P(None, "tensor"),
            P(None, "tensor"),
            P(None, "tensor"),
        ),
        out_specs=(P("dp"), P("dp", "tensor"), P("dp", "tensor")),
        check_vma=False,
    )
```

```python
import jax
import jax.numpy as jnp
from jax import lax
from jax.experimental import pallas as pl
from jax.experimental.pallas import tpu as pltpu
from jax.sharding import PartitionSpec as P

D = 8192
F32 = jnp.float32
BF16 = jnp.bfloat16

PLACES = [(zh, zl, c) for zh in range(4) for zl in range(4) for c in range(2)]
CORES = [(d, d ^ 1) for d in range(32)]
FAR = [[8 * h + 2 * l + c for h in range(4)] for l in range(4) for c in range(2)]
def index(zh, zl, c):
    return 8 * zh + 2 * zl + c


def near_step(k):
    return [(index(zh, zl, c), index(zh, zl ^ k, c)) for zh, zl, c in PLACES]


def ring_step(k):
    return [(d, (d + (2 - 4 * (d % 2)) * k) % 32) for d in range(32)]


FAR_STEP = [(index(zh, zl, c), index((zh - 1 + 2 * c) % 4, zl, c)) for zh, zl, c in PLACES]


HOME = [
    (index(zh, zl, c) * 16 + 4 * x + y, index(zh, y, c) * 16 + 4 * x + zl)
    for zh, zl, c in PLACES
    for x in range(4)
    for y in range(4)
]


def swap_all(x, axis, groups=None):
    return lax.all_to_all(x, axis, split_axis=0, concat_axis=0, tiled=True, axis_index_groups=groups)


def call(body, name, flops, out_shape, scalars, *arrays):
    vmem = pl.BlockSpec(memory_space=pltpu.VMEM)
    smem = pl.BlockSpec(memory_space=pltpu.SMEM)
    return pl.pallas_call(
        body,
        out_shape=out_shape,
        in_specs=[smem] * len(scalars) + [vmem] * len(arrays),
        out_specs=jax.tree.map(lambda _: vmem, out_shape),
        compiler_params=pltpu.CompilerParams(vmem_limit_bytes=32 << 20),
        cost_estimate=pl.CostEstimate(flops=flops, bytes_accessed=2 << 20, transcendentals=0),
        name=name,
    )(*scalars, *arrays)


def halves(x):
    high = x.astype(BF16).astype(F32)
    return high, x - high


def forward_body(rows, up, down, normed, preact, hidden, pieces):
    x = rows[...].astype(F32)
    mean = jnp.mean(x * x, axis=-1, keepdims=True)
    normed[...] = (x * lax.rsqrt(mean + 1e-05)).astype(BF16)
    pre = lax.dot_general(normed[...], up[...], (((1,), (1,)), ((), ())), preferred_element_type=F32)
    preact[...] = pre
    units = (pre * jax.nn.sigmoid(pre)).astype(BF16)
    hidden[...] = units
    for pair in range(8):
        columns = slice(pair * 256, pair * 256 + 256)
        part = jnp.dot(units, down[:, columns], preferred_element_type=F32).astype(BF16)
        pieces[2 * pair] = part[:, :128]
        pieces[2 * pair + 1] = part[:, 128:]


def head_body(
    place_ref, student, mixed, own, near1, near2, near3, mine, pair, far, half, got, out
):
    zh, zl, core, tensor = place_ref[0], place_ref[1], place_ref[2], place_ref[4]
    mixed_sum = mixed[0].astype(F32)
    for t in range(1, 16):
        mixed_sum += mixed[t].astype(F32)
    block = student[:, pl.ds(pl.multiple_of(tensor * 128, 128), 128)].astype(F32)
    updated = (block + mixed_sum).astype(BF16)
    rows = jnp.concatenate([own[...], near1[...], near2[...], near3[...]], axis=0)

    def in_order(of_core, of_other):
        return jnp.where(core == 0, of_core, of_other), jnp.where(core == 0, of_other, of_core)

    def opposite(column_core):
        held = jnp.where(core == column_core, half[0], half[1])
        other = jnp.where(core == column_core, got[1, 256:], got[0, 256:])
        return jnp.concatenate(in_order(held, other), axis=0)

    side_step = jnp.where(core == 0, 1, 3)
    for step, sides in (
        (0, in_order(mine[...], pair[...])),
        (side_step, in_order(far[0], far[1])),
        (4 - side_step, in_order(got[1, :256], got[0, :256])),
        (2, (opposite(0), opposite(1))),
    ):
        for side, columns in enumerate(sides):
            part = jnp.dot(rows, columns, preferred_element_type=F32).astype(BF16)
            for near in range(4):
                piece = (zh + step) % 4 * 4 + (zl ^ near)
                out[piece, :, side * 256 : side * 256 + 256] = part[near * 128 : near * 128 + 128]
    for t in range(16):
        out[t, :, 512:] = updated


def head_sum_body(got, head, updated):
    total = got[0, :, :512].astype(F32)
    for t in range(1, 16):
        total += got[t, :, :512].astype(F32)
    head[...] = total.astype(BF16)
    for t in range(16):
        updated[:, t * 128 : t * 128 + 128] = got[t, :, 512:]


def project_body(updated, proj, out):
    out[...] = jnp.dot(updated[...], proj[...], preferred_element_type=F32)


def residue_body(scale_ref, length_ref, owners, projected, resid, head, proj, pieces):
    scale, length = scale_ref[0], length_ref[0]
    target = (resid[...].astype(F32) + head[...].astype(F32)).astype(BF16)
    residue = projected[...] - target.astype(F32)
    row = lax.broadcasted_iota(jnp.int32, (128, 1), 0)
    live = (row < length).astype(F32)
    squares = live * jnp.sum(residue * residue, axis=-1, keepdims=True)
    owner = lax.broadcasted_iota(jnp.int32, (128, 128), 1)
    losses = jnp.sum(jnp.where(owners[...] == owner, squares, 0.0), axis=0, keepdims=True)
    high, low = halves(losses)
    side_row = lax.broadcasted_iota(jnp.int32, (16, 128), 0)
    side = jnp.where(side_row == 0, high, jnp.where(side_row == 1, low, 0.0)).astype(BF16)
    cotangent = (2.0 * scale * live * residue).astype(BF16)
    for pair in range(8):
        part = lax.dot_general(
            cotangent,
            proj[pair * 256 : pair * 256 + 256],
            (((1,), (1,)), ((), ())),
            preferred_element_type=F32,
        ).astype(BF16)
        pieces[2 * pair, :128] = part[:, :128]
        pieces[2 * pair + 1, :128] = part[:, 128:]
    for t in range(16):
        pieces[t, 128:] = side


def back_sum_body(got, out, losses):
    total = got[0].astype(F32)
    for t in range(1, 16):
        total += got[t].astype(F32)
    block = total[:128].astype(BF16)
    for t in range(16):
        out[t] = block
    losses[...] = total[128:129] + total[129:130]


def grad_body(place_ref, losses, blocks, hidden, preact, normed, down, mine, other):
    zl, core, source = place_ref[1], place_ref[2], place_ref[3]
    out_grad = jnp.concatenate([blocks[t] for t in range(16)], axis=1)
    hidden_grad = lax.dot_general(
        out_grad, down[...], (((1,), (1,)), ((), ())), preferred_element_type=F32
    )
    pre = preact[...]
    gate_sig = jax.nn.sigmoid(pre)
    pre_grad = hidden_grad * gate_sig * (1.0 + pre * (1.0 - gate_sig))
    up_left = pre_grad.T.astype(BF16)
    down_left = hidden[...].astype(F32).T.astype(BF16)
    lane = lax.broadcasted_iota(jnp.int32, (176, 128), 1)
    loss_lane = lax.broadcasted_iota(jnp.int32, (1, 128), 1)
    side_lane = lax.broadcasted_iota(jnp.int32, (16, 128), 1)
    for pair in range(8):
        columns = slice(pair * 256, pair * 256 + 256)
        up_pair = jnp.dot(up_left, normed[:, columns], preferred_element_type=F32)
        down_pair = jnp.dot(down_left, out_grad[:, columns], preferred_element_type=F32)
        for half in range(2):
            chip = 2 * pair + half
            ahead = (chip % 4 - zl + 4) % 4
            back = (4 - ahead) % 4
            own_piece = jnp.where(core == 0, ahead, back) * 4 + chip // 4
            other_piece = jnp.where(core == 0, back, ahead) * 4 + chip // 4
            up = up_pair[:, half * 128 : half * 128 + 128]
            below = down_pair[:, half * 128 : half * 128 + 128]
            even = jnp.where(lane < 64, up, pltpu.roll(below, 64, 1))
            odd = jnp.where(lane < 64, pltpu.roll(up, 64, 1), below)
            mine[own_piece, :176] = jnp.where(core == 0, even, odd).astype(BF16)
            other[other_piece, :176] = jnp.where(core == 0, odd, even).astype(BF16)
            for out, piece, owner in (
                (mine, own_piece, 2 * chip + core),
                (other, other_piece, 2 * chip + 1 - core),
            ):
                loss = jnp.where(loss_lane == owner, losses[...], 0.0)
                high, low = halves(jnp.sum(loss, axis=1, keepdims=True))
                side = jnp.where(
                    side_lane == 2 * source, high, jnp.where(side_lane == 2 * source + 1, low, 0.0)
                )
                out[piece, 176:] = side.astype(BF16)


def finish_body(scale_ref, got, loss, up, down):
    total = got[0].astype(F32)
    for zh in range(1, 4):
        total += got[zh].astype(F32)
    sums = jnp.sum(total[176:177], axis=1, keepdims=True)
    loss[...] = sums * scale_ref[0]
    grads = total[:176].T
    up[...] = grads[:64]
    down[...] = grads[64:]


def on_device(
    resid,
    context,
    out_weight,
    owners,
    query_lengths,
    student_rows,
    up_weight,
    down_weight,
    proj_weight,
):
    shape = jax.ShapeDtypeStruct
    dp = lax.axis_index("dp")
    place = jnp.stack([dp // 8, dp // 2 % 4, dp % 2, dp, lax.axis_index("tensor")]).astype(jnp.int32)
    loss_scale = 32.0 / (jnp.sum(query_lengths).astype(F32) * D)
    own_length = lax.dynamic_slice_in_dim(query_lengths, dp, 1)

    rows = [context] + [lax.ppermute(context, "dp", near_step(k)) for k in (1, 2, 3)]
    pair = lax.ppermute(out_weight, "dp", CORES)
    far = lax.ppermute(jnp.stack([out_weight, pair]), "dp", FAR_STEP)

    normed, preact, hidden, mixed = call(
        forward_body,
        "forward",
        4 * 128 * 2048 * 176,
        (
            shape((128, 2048), BF16),
            shape((128, 176), F32),
            shape((128, 176), BF16),
            shape((16, 128, 128), BF16),
        ),
        (),
        student_rows,
        up_weight.T,
        down_weight.T,
    )
    rows, far, mixed = lax.optimization_barrier((rows, far, mixed))
    half = lax.dynamic_slice_in_dim(far, dp % 2 * 128, 128, axis=1)
    half = lax.ppermute(half, "dp", FAR_STEP)
    mixed = swap_all(mixed, "tensor")
    half, mixed = lax.optimization_barrier((half, mixed))
    got = lax.ppermute(jnp.concatenate([far, half], axis=1), "dp", CORES)
    parts = call(
        head_body,
        "head_parts",
        2 * 512 * 2048 * 256,
        shape((16, 128, 640), BF16),
        (place,),
        student_rows,
        mixed,
        *rows,
        out_weight,
        pair,
        far,
        half,
        got,
    )
    head, updated = call(
        head_sum_body,
        "head_sum",
        16 * 128 * 512,
        (shape((128, 512), BF16), shape((128, 2048), BF16)),
        (),
        swap_all(parts, "tensor"),
    )
    head = lax.ppermute(head, ("dp", "tensor"), HOME)
    projected = call(
        project_body, "project", 2 * 128 * 2048 * 512, shape((128, 512), F32), (), updated, proj_weight
    )
    pieces = call(
        residue_body,
        "residue",
        2 * 128 * 2048 * 512,
        shape((16, 144, 128), BF16),
        (jnp.reshape(loss_scale, (1,)), own_length),
        owners,
        projected,
        resid,
        head,
        proj_weight,
    )
    blocks, losses = call(
        back_sum_body,
        "back_sum",
        16 * 128 * 128,
        (shape((16, 128, 128), BF16), shape((1, 128), F32)),
        (),
        swap_all(pieces, "tensor"),
    )
    mine, other = call(
        grad_body,
        "grad_terms",
        6 * 128 * 2048 * 176,
        (shape((16, 192, 128), BF16),) * 2,
        (place,),
        losses,
        swap_all(blocks, "tensor"),
        hidden,
        preact,
        normed,
        down_weight.T,
    )
    pair = (mine.astype(F32) + lax.ppermute(other, "dp", CORES).astype(F32)).astype(BF16)
    pair = pair.reshape(4, 4, 192, 128)
    near = pair[0].astype(F32)
    for k, step in ((1, 1), (3, -1), (2, 2)):
        near += lax.ppermute(pair[k], "dp", ring_step(step)).astype(F32)
    near = near.astype(BF16)
    grad = shape((64, 176), F32)
    loss, grad_up, grad_down = call(
        finish_body,
        "finish",
        4 * 192 * 128,
        (shape((1, 1), F32), grad, grad),
        (jnp.reshape(loss_scale, (1,)),),
        swap_all(near, "dp", FAR),
    )
    return (jnp.reshape(loss, (1,)), grad_up, grad_down)


def solution(mesh):
    return jax.shard_map(
        on_device,
        mesh=mesh,
        in_specs=(
            P("dp", "tensor"),
            P("dp", "tensor"),
            P("tensor", "dp"),
            P("dp", None),
            P(),
            P("dp", None),
            P(None, "tensor"),
            P(None, "tensor"),
            P(None, "tensor"),
        ),
        out_specs=(P("dp"), P("dp", "tensor"), P("dp", "tensor")),
        check_vma=False,
    )
```

```python
import jax
import jax.numpy as jnp
from jax import lax
from jax.experimental import pallas as pl
from jax.experimental.pallas import tpu as pltpu
from jax.sharding import PartitionSpec as P

D = 8192
F32 = jnp.float32
BF16 = jnp.bfloat16

PLACES = [(zh, zl, c) for zh in range(4) for zl in range(4) for c in range(2)]
CORES = [(d, d ^ 1) for d in range(32)]
FAR = [[8 * h + 2 * l + c for h in range(4)] for l in range(4) for c in range(2)]
def index(zh, zl, c):
    return 8 * zh + 2 * zl + c


def near_step(k):
    return [(index(zh, zl, c), index(zh, zl ^ k, c)) for zh, zl, c in PLACES]


def ring_step(k):
    return [(d, (d + (2 - 4 * (d % 2)) * k) % 32) for d in range(32)]


FAR_STEP = [(index(zh, zl, c), index((zh - 1 + 2 * c) % 4, zl, c)) for zh, zl, c in PLACES]


HOME = [
    (index(zh, zl, c) * 16 + 4 * x + y, index(zh, y, c) * 16 + 4 * x + zl)
    for zh, zl, c in PLACES
    for x in range(4)
    for y in range(4)
]


def swap_all(x, axis, groups=None):
    return lax.all_to_all(x, axis, split_axis=0, concat_axis=0, tiled=True, axis_index_groups=groups)


def call(body, name, flops, out_shape, scalars, *arrays):
    vmem = pl.BlockSpec(memory_space=pltpu.VMEM)
    smem = pl.BlockSpec(memory_space=pltpu.SMEM)
    return pl.pallas_call(
        body,
        out_shape=out_shape,
        in_specs=[smem] * len(scalars) + [vmem] * len(arrays),
        out_specs=jax.tree.map(lambda _: vmem, out_shape),
        compiler_params=pltpu.CompilerParams(vmem_limit_bytes=32 << 20),
        cost_estimate=pl.CostEstimate(flops=flops, bytes_accessed=2 << 20, transcendentals=0),
        name=name,
    )(*scalars, *arrays)


def halves(x):
    high = x.astype(BF16).astype(F32)
    return high, x - high


def forward_body(rows, up, down, normed, preact, hidden, pieces):
    x = rows[...].astype(F32)
    mean = jnp.mean(x * x, axis=-1, keepdims=True)
    normed[...] = (x * lax.rsqrt(mean + 1e-05)).astype(BF16)
    pre = lax.dot_general(normed[...], up[...], (((1,), (1,)), ((), ())), preferred_element_type=F32)
    preact[...] = pre
    units = (pre * jax.nn.sigmoid(pre)).astype(BF16)
    hidden[...] = units
    for pair in range(8):
        columns = slice(pair * 256, pair * 256 + 256)
        part = jnp.dot(units, down[:, columns], preferred_element_type=F32).astype(BF16)
        pieces[2 * pair] = part[:, :128]
        pieces[2 * pair + 1] = part[:, 128:]


def head_body(
    place_ref, student, mixed, own, near1, near2, near3, mine, pair, far, half, got, out
):
    zh, zl, core, tensor = place_ref[0], place_ref[1], place_ref[2], place_ref[4]
    mixed_sum = mixed[0].astype(F32)
    for t in range(1, 16):
        mixed_sum += mixed[t].astype(F32)
    block = student[:, pl.ds(pl.multiple_of(tensor * 128, 128), 128)].astype(F32)
    updated = (block + mixed_sum).astype(BF16)
    rows = jnp.concatenate([own[...], near1[...], near2[...], near3[...]], axis=0)

    def in_order(of_core, of_other):
        return jnp.where(core == 0, of_core, of_other), jnp.where(core == 0, of_other, of_core)

    def opposite(column_core):
        held = jnp.where(core == column_core, half[0], half[1])
        other = jnp.where(core == column_core, got[1, 256:], got[0, 256:])
        return jnp.concatenate(in_order(held, other), axis=0)

    side_step = jnp.where(core == 0, 1, 3)
    for step, sides in (
        (0, in_order(mine[...], pair[...])),
        (side_step, in_order(far[0], far[1])),
        (4 - side_step, in_order(got[1, :256], got[0, :256])),
        (2, (opposite(0), opposite(1))),
    ):
        for side, columns in enumerate(sides):
            part = jnp.dot(rows, columns, preferred_element_type=F32).astype(BF16)
            for near in range(4):
                piece = (zh + step) % 4 * 4 + (zl ^ near)
                out[piece, :, side * 256 : side * 256 + 256] = part[near * 128 : near * 128 + 128]
    for t in range(16):
        out[t, :, 512:] = updated


def head_sum_body(got, head, updated):
    total = got[0, :, :512].astype(F32)
    for t in range(1, 16):
        total += got[t, :, :512].astype(F32)
    head[...] = total.astype(BF16)
    for t in range(16):
        updated[:, t * 128 : t * 128 + 128] = got[t, :, 512:]


def project_body(updated, proj, out):
    out[...] = jnp.dot(updated[...], proj[...], preferred_element_type=F32)


def residue_body(scale_ref, length_ref, owners, projected, resid, head, proj, pieces):
    scale, length = scale_ref[0], length_ref[0]
    target = (resid[...].astype(F32) + head[...].astype(F32)).astype(BF16)
    residue = projected[...] - target.astype(F32)
    row = lax.broadcasted_iota(jnp.int32, (128, 1), 0)
    live = (row < length).astype(F32)
    squares = live * jnp.sum(residue * residue, axis=-1, keepdims=True)
    owner = lax.broadcasted_iota(jnp.int32, (128, 128), 1)
    losses = jnp.sum(jnp.where(owners[...] == owner, squares, 0.0), axis=0, keepdims=True)
    high, low = halves(losses)
    side_row = lax.broadcasted_iota(jnp.int32, (16, 128), 0)
    side = jnp.where(side_row == 0, high, jnp.where(side_row == 1, low, 0.0)).astype(BF16)
    cotangent = (2.0 * scale * live * residue).astype(BF16)
    for pair in range(8):
        part = lax.dot_general(
            cotangent,
            proj[pair * 256 : pair * 256 + 256],
            (((1,), (1,)), ((), ())),
            preferred_element_type=F32,
        ).astype(BF16)
        pieces[2 * pair, :128] = part[:, :128]
        pieces[2 * pair + 1, :128] = part[:, 128:]
    for t in range(16):
        pieces[t, 128:] = side


def back_sum_body(got, out, losses):
    total = got[0].astype(F32)
    for t in range(1, 16):
        total += got[t].astype(F32)
    block = total[:128].astype(BF16)
    for t in range(16):
        out[t] = block
    losses[...] = total[128:129] + total[129:130]


def grad_body(place_ref, losses, blocks, hidden, preact, normed, down, mine, other):
    zl, core, source = place_ref[1], place_ref[2], place_ref[3]
    out_grad = jnp.concatenate([blocks[t] for t in range(16)], axis=1)
    hidden_grad = lax.dot_general(
        out_grad, down[...], (((1,), (1,)), ((), ())), preferred_element_type=F32
    )
    pre = preact[...]
    gate_sig = jax.nn.sigmoid(pre)
    pre_grad = hidden_grad * gate_sig * (1.0 + pre * (1.0 - gate_sig))
    up_left = pre_grad.T.astype(BF16)
    down_left = hidden[...].astype(F32).T.astype(BF16)
    lane = lax.broadcasted_iota(jnp.int32, (176, 128), 1)
    loss_lane = lax.broadcasted_iota(jnp.int32, (1, 128), 1)
    side_lane = lax.broadcasted_iota(jnp.int32, (16, 128), 1)
    for pair in range(8):
        columns = slice(pair * 256, pair * 256 + 256)
        up_pair = jnp.dot(up_left, normed[:, columns], preferred_element_type=F32)
        down_pair = jnp.dot(down_left, out_grad[:, columns], preferred_element_type=F32)
        for half in range(2):
            chip = 2 * pair + half
            ahead = (chip % 4 - zl + 4) % 4
            back = (4 - ahead) % 4
            own_piece = jnp.where(core == 0, ahead, back) * 4 + chip // 4
            other_piece = jnp.where(core == 0, back, ahead) * 4 + chip // 4
            up = up_pair[:, half * 128 : half * 128 + 128]
            below = down_pair[:, half * 128 : half * 128 + 128]
            even = jnp.where(lane < 64, up, pltpu.roll(below, 64, 1))
            odd = jnp.where(lane < 64, pltpu.roll(up, 64, 1), below)
            mine[own_piece, :176] = jnp.where(core == 0, even, odd).astype(BF16)
            other[other_piece, :176] = jnp.where(core == 0, odd, even).astype(BF16)
            for out, piece, owner in (
                (mine, own_piece, 2 * chip + core),
                (other, other_piece, 2 * chip + 1 - core),
            ):
                loss = jnp.where(loss_lane == owner, losses[...], 0.0)
                high, low = halves(jnp.sum(loss, axis=1, keepdims=True))
                side = jnp.where(
                    side_lane == 2 * source, high, jnp.where(side_lane == 2 * source + 1, low, 0.0)
                )
                out[piece, 176:] = side.astype(BF16)


def finish_body(scale_ref, got, loss, up, down):
    total = got[0].astype(F32)
    for zh in range(1, 4):
        total += got[zh].astype(F32)
    sums = jnp.sum(total[176:177], axis=1, keepdims=True)
    loss[...] = sums * scale_ref[0]
    grads = total[:176].T
    up[...] = grads[:64]
    down[...] = grads[64:]


def on_device(
    resid,
    context,
    out_weight,
    owners,
    query_lengths,
    student_rows,
    up_weight,
    down_weight,
    proj_weight,
):
    shape = jax.ShapeDtypeStruct
    dp = lax.axis_index("dp")
    place = jnp.stack([dp // 8, dp // 2 % 4, dp % 2, dp, lax.axis_index("tensor")]).astype(jnp.int32)
    loss_scale = 32.0 / (jnp.sum(query_lengths).astype(F32) * D)
    own_length = lax.dynamic_slice_in_dim(query_lengths, dp, 1)

    rows = [context] + [lax.ppermute(context, "dp", near_step(k)) for k in (1, 2, 3)]
    pair = lax.ppermute(out_weight, "dp", CORES)
    far = lax.ppermute(jnp.stack([out_weight, pair]), "dp", FAR_STEP)

    normed, preact, hidden, mixed = call(
        forward_body,
        "forward",
        4 * 128 * 2048 * 176,
        (
            shape((128, 2048), BF16),
            shape((128, 176), F32),
            shape((128, 176), BF16),
            shape((16, 128, 128), BF16),
        ),
        (),
        student_rows,
        up_weight.T,
        down_weight.T,
    )
    rows, far, mixed = lax.optimization_barrier((rows, far, mixed))
    half = lax.dynamic_slice_in_dim(far, dp % 2 * 128, 128, axis=1)
    half = lax.ppermute(half, "dp", FAR_STEP)
    got = lax.ppermute(jnp.concatenate([far, half], axis=1), "dp", CORES)
    mixed = swap_all(mixed, "tensor")
    got, mixed = lax.optimization_barrier((got, mixed))
    parts = call(
        head_body,
        "head_parts",
        2 * 512 * 2048 * 256,
        shape((16, 128, 640), BF16),
        (place,),
        student_rows,
        mixed,
        *rows,
        out_weight,
        pair,
        far,
        half,
        got,
    )
    head, updated = call(
        head_sum_body,
        "head_sum",
        16 * 128 * 512,
        (shape((128, 512), BF16), shape((128, 2048), BF16)),
        (),
        swap_all(parts, "tensor"),
    )
    head = lax.ppermute(head, ("dp", "tensor"), HOME)
    projected = call(
        project_body, "project", 2 * 128 * 2048 * 512, shape((128, 512), F32), (), updated, proj_weight
    )
    pieces = call(
        residue_body,
        "residue",
        2 * 128 * 2048 * 512,
        shape((16, 144, 128), BF16),
        (jnp.reshape(loss_scale, (1,)), own_length),
        owners,
        projected,
        resid,
        head,
        proj_weight,
    )
    blocks, losses = call(
        back_sum_body,
        "back_sum",
        16 * 128 * 128,
        (shape((16, 128, 128), BF16), shape((1, 128), F32)),
        (),
        swap_all(pieces, "tensor"),
    )
    mine, other = call(
        grad_body,
        "grad_terms",
        6 * 128 * 2048 * 176,
        (shape((16, 192, 128), BF16),) * 2,
        (place,),
        losses,
        swap_all(blocks, "tensor"),
        hidden,
        preact,
        normed,
        down_weight.T,
    )
    pair = (mine.astype(F32) + lax.ppermute(other, "dp", CORES).astype(F32)).astype(BF16)
    pair = pair.reshape(4, 4, 192, 128)
    near = pair[0].astype(F32)
    for k, step in ((1, 1), (3, -1), (2, 2)):
        near += lax.ppermute(pair[k], "dp", ring_step(step)).astype(F32)
    near = near.astype(BF16)
    grad = shape((64, 176), F32)
    loss, grad_up, grad_down = call(
        finish_body,
        "finish",
        4 * 192 * 128,
        (shape((1, 1), F32), grad, grad),
        (jnp.reshape(loss_scale, (1,)),),
        swap_all(near, "dp", FAR),
    )
    return (jnp.reshape(loss, (1,)), grad_up, grad_down)


def solution(mesh):
    return jax.shard_map(
        on_device,
        mesh=mesh,
        in_specs=(
            P("dp", "tensor"),
            P("dp", "tensor"),
            P("tensor", "dp"),
            P("dp", None),
            P(),
            P("dp", None),
            P(None, "tensor"),
            P(None, "tensor"),
            P(None, "tensor"),
        ),
        out_specs=(P("dp"), P("dp", "tensor"), P("dp", "tensor")),
        check_vma=False,
    )
```

```python
import jax
import jax.numpy as jnp
from jax import lax
from jax.experimental import pallas as pl
from jax.experimental.pallas import tpu as pltpu
from jax.sharding import PartitionSpec as P

D = 8192
F32 = jnp.float32
BF16 = jnp.bfloat16

PLACES = [(zh, zl, c) for zh in range(4) for zl in range(4) for c in range(2)]
CORES = [(d, d ^ 1) for d in range(32)]
FAR = [[8 * h + 2 * l + c for h in range(4)] for l in range(4) for c in range(2)]
def index(zh, zl, c):
    return 8 * zh + 2 * zl + c


def ring_step(k):
    return [(d, (d + (2 - 4 * (d % 2)) * k) % 32) for d in range(32)]


FAR_STEP = [(index(zh, zl, c), index((zh - 1 + 2 * c) % 4, zl, c)) for zh, zl, c in PLACES]


NEAR = (0, 1, -1, 2)


def home_of(zh, zl, c, x, y):
    chip = (4 * zh + zl + NEAR[y] * (1 - 2 * c)) % 16
    return (2 * chip + c) * 16 + 4 * x + zl


HOME = [
    (index(zh, zl, c) * 16 + 4 * x + y, home_of(zh, zl, c, x, y))
    for zh, zl, c in PLACES
    for x in range(4)
    for y in range(4)
]


def swap_all(x, axis, groups=None):
    return lax.all_to_all(x, axis, split_axis=0, concat_axis=0, tiled=True, axis_index_groups=groups)


def call(body, name, flops, out_shape, scalars, *arrays):
    vmem = pl.BlockSpec(memory_space=pltpu.VMEM)
    smem = pl.BlockSpec(memory_space=pltpu.SMEM)
    return pl.pallas_call(
        body,
        out_shape=out_shape,
        in_specs=[smem] * len(scalars) + [vmem] * len(arrays),
        out_specs=jax.tree.map(lambda _: vmem, out_shape),
        compiler_params=pltpu.CompilerParams(vmem_limit_bytes=32 << 20),
        cost_estimate=pl.CostEstimate(flops=flops, bytes_accessed=2 << 20, transcendentals=0),
        name=name,
    )(*scalars, *arrays)


def halves(x):
    high = x.astype(BF16).astype(F32)
    return high, x - high


def forward_body(rows, up, down, normed, preact, hidden, pieces):
    x = rows[...].astype(F32)
    mean = jnp.mean(x * x, axis=-1, keepdims=True)
    normed[...] = (x * lax.rsqrt(mean + 1e-05)).astype(BF16)
    pre = lax.dot_general(normed[...], up[...], (((1,), (1,)), ((), ())), preferred_element_type=F32)
    preact[...] = pre
    units = (pre * jax.nn.sigmoid(pre)).astype(BF16)
    hidden[...] = units
    for pair in range(8):
        columns = slice(pair * 256, pair * 256 + 256)
        part = jnp.dot(units, down[:, columns], preferred_element_type=F32).astype(BF16)
        pieces[2 * pair] = part[:, :128]
        pieces[2 * pair + 1] = part[:, 128:]


def head_body(
    place_ref, student, mixed, own, near1, near2, near3, mine, pair, far, half, got, out
):
    zh, core, tensor = place_ref[0], place_ref[2], place_ref[4]
    mixed_sum = mixed[0].astype(F32)
    for t in range(1, 16):
        mixed_sum += mixed[t].astype(F32)
    block = student[:, pl.ds(pl.multiple_of(tensor * 128, 128), 128)].astype(F32)
    updated = (block + mixed_sum).astype(BF16)
    rows = jnp.concatenate([own[...], near1[...], near2[...], near3[...]], axis=0)

    def in_order(of_core, of_other):
        return jnp.where(core == 0, of_core, of_other), jnp.where(core == 0, of_other, of_core)

    def opposite(column_core):
        held = jnp.where(core == column_core, half[0], half[1])
        other = jnp.where(core == column_core, got[1, 256:], got[0, 256:])
        return jnp.concatenate(in_order(held, other), axis=0)

    side_step = jnp.where(core == 0, 1, 3)
    for step, sides in (
        (0, in_order(mine[...], pair[...])),
        (side_step, in_order(far[0], far[1])),
        (4 - side_step, in_order(got[1, :256], got[0, :256])),
        (2, (opposite(0), opposite(1))),
    ):
        for side, columns in enumerate(sides):
            part = jnp.dot(rows, columns, preferred_element_type=F32).astype(BF16)
            for near in range(4):
                piece = (zh + step) % 4 * 4 + near
                out[piece, :, side * 256 : side * 256 + 256] = part[near * 128 : near * 128 + 128]
    for t in range(16):
        out[t, :, 512:] = updated


def head_sum_body(got, head, updated):
    total = got[0, :, :512].astype(F32)
    for t in range(1, 16):
        total += got[t, :, :512].astype(F32)
    head[...] = total.astype(BF16)
    for t in range(16):
        updated[:, t * 128 : t * 128 + 128] = got[t, :, 512:]


def project_body(updated, proj, out):
    out[...] = jnp.dot(updated[...], proj[...], preferred_element_type=F32)


def residue_body(scale_ref, length_ref, owners, projected, resid, head, proj, pieces):
    scale, length = scale_ref[0], length_ref[0]
    target = (resid[...].astype(F32) + head[...].astype(F32)).astype(BF16)
    residue = projected[...] - target.astype(F32)
    row = lax.broadcasted_iota(jnp.int32, (128, 1), 0)
    live = (row < length).astype(F32)
    squares = live * jnp.sum(residue * residue, axis=-1, keepdims=True)
    owner = lax.broadcasted_iota(jnp.int32, (128, 128), 1)
    losses = jnp.sum(jnp.where(owners[...] == owner, squares, 0.0), axis=0, keepdims=True)
    high, low = halves(losses)
    side_row = lax.broadcasted_iota(jnp.int32, (16, 128), 0)
    side = jnp.where(side_row == 0, high, jnp.where(side_row == 1, low, 0.0)).astype(BF16)
    cotangent = (2.0 * scale * live * residue).astype(BF16)
    for pair in range(8):
        part = lax.dot_general(
            cotangent,
            proj[pair * 256 : pair * 256 + 256],
            (((1,), (1,)), ((), ())),
            preferred_element_type=F32,
        ).astype(BF16)
        pieces[2 * pair, :128] = part[:, :128]
        pieces[2 * pair + 1, :128] = part[:, 128:]
    for t in range(16):
        pieces[t, 128:] = side


def back_sum_body(got, out, losses):
    total = got[0].astype(F32)
    for t in range(1, 16):
        total += got[t].astype(F32)
    block = total[:128].astype(BF16)
    for t in range(16):
        out[t] = block
    losses[...] = total[128:129] + total[129:130]


def grad_body(place_ref, losses, blocks, hidden, preact, normed, down, mine, other):
    zl, core, source = place_ref[1], place_ref[2], place_ref[3]
    out_grad = jnp.concatenate([blocks[t] for t in range(16)], axis=1)
    hidden_grad = lax.dot_general(
        out_grad, down[...], (((1,), (1,)), ((), ())), preferred_element_type=F32
    )
    pre = preact[...]
    gate_sig = jax.nn.sigmoid(pre)
    pre_grad = hidden_grad * gate_sig * (1.0 + pre * (1.0 - gate_sig))
    up_left = pre_grad.T.astype(BF16)
    down_left = hidden[...].astype(F32).T.astype(BF16)
    lane = lax.broadcasted_iota(jnp.int32, (176, 128), 1)
    loss_lane = lax.broadcasted_iota(jnp.int32, (1, 128), 1)
    side_lane = lax.broadcasted_iota(jnp.int32, (16, 128), 1)
    for pair in range(8):
        columns = slice(pair * 256, pair * 256 + 256)
        up_pair = jnp.dot(up_left, normed[:, columns], preferred_element_type=F32)
        down_pair = jnp.dot(down_left, out_grad[:, columns], preferred_element_type=F32)
        for half in range(2):
            chip = 2 * pair + half
            ahead = (chip % 4 - zl + 4) % 4
            back = (4 - ahead) % 4
            own_piece = jnp.where(core == 0, ahead, back) * 4 + chip // 4
            other_piece = jnp.where(core == 0, back, ahead) * 4 + chip // 4
            up = up_pair[:, half * 128 : half * 128 + 128]
            below = down_pair[:, half * 128 : half * 128 + 128]
            even = jnp.where(lane < 64, up, pltpu.roll(below, 64, 1))
            odd = jnp.where(lane < 64, pltpu.roll(up, 64, 1), below)
            mine[own_piece, :176] = jnp.where(core == 0, even, odd).astype(BF16)
            other[other_piece, :176] = jnp.where(core == 0, odd, even).astype(BF16)
            for out, piece, owner in (
                (mine, own_piece, 2 * chip + core),
                (other, other_piece, 2 * chip + 1 - core),
            ):
                loss = jnp.where(loss_lane == owner, losses[...], 0.0)
                high, low = halves(jnp.sum(loss, axis=1, keepdims=True))
                side = jnp.where(
                    side_lane == 2 * source, high, jnp.where(side_lane == 2 * source + 1, low, 0.0)
                )
                out[piece, 176:] = side.astype(BF16)


def finish_body(scale_ref, got, loss, up, down):
    total = got[0].astype(F32)
    for zh in range(1, 4):
        total += got[zh].astype(F32)
    sums = jnp.sum(total[176:177], axis=1, keepdims=True)
    loss[...] = sums * scale_ref[0]
    grads = total[:176].T
    up[...] = grads[:64]
    down[...] = grads[64:]


def on_device(
    resid,
    context,
    out_weight,
    owners,
    query_lengths,
    student_rows,
    up_weight,
    down_weight,
    proj_weight,
):
    shape = jax.ShapeDtypeStruct
    dp = lax.axis_index("dp")
    place = jnp.stack([dp // 8, dp // 2 % 4, dp % 2, dp, lax.axis_index("tensor")]).astype(jnp.int32)
    loss_scale = 32.0 / (jnp.sum(query_lengths).astype(F32) * D)
    own_length = lax.dynamic_slice_in_dim(query_lengths, dp, 1)

    rows = [context] + [lax.ppermute(context, "dp", ring_step(-k)) for k in NEAR[1:]]
    pair = lax.ppermute(out_weight, "dp", CORES)
    far = lax.ppermute(jnp.stack([out_weight, pair]), "dp", FAR_STEP)

    normed, preact, hidden, mixed = call(
        forward_body,
        "forward",
        4 * 128 * 2048 * 176,
        (
            shape((128, 2048), BF16),
            shape((128, 176), F32),
            shape((128, 176), BF16),
            shape((16, 128, 128), BF16),
        ),
        (),
        student_rows,
        up_weight.T,
        down_weight.T,
    )
    rows, far, mixed = lax.optimization_barrier((rows, far, mixed))
    half = lax.dynamic_slice_in_dim(far, dp % 2 * 128, 128, axis=1)
    half = lax.ppermute(half, "dp", FAR_STEP)
    got = lax.ppermute(jnp.concatenate([far, half], axis=1), "dp", CORES)
    mixed = swap_all(mixed, "tensor")
    got, mixed = lax.optimization_barrier((got, mixed))
    parts = call(
        head_body,
        "head_parts",
        2 * 512 * 2048 * 256,
        shape((16, 128, 640), BF16),
        (place,),
        student_rows,
        mixed,
        *rows,
        out_weight,
        pair,
        far,
        half,
        got,
    )
    head, updated = call(
        head_sum_body,
        "head_sum",
        16 * 128 * 512,
        (shape((128, 512), BF16), shape((128, 2048), BF16)),
        (),
        swap_all(parts, "tensor"),
    )
    head = lax.ppermute(head, ("dp", "tensor"), HOME)
    projected = call(
        project_body, "project", 2 * 128 * 2048 * 512, shape((128, 512), F32), (), updated, proj_weight
    )
    pieces = call(
        residue_body,
        "residue",
        2 * 128 * 2048 * 512,
        shape((16, 144, 128), BF16),
        (jnp.reshape(loss_scale, (1,)), own_length),
        owners,
        projected,
        resid,
        head,
        proj_weight,
    )
    blocks, losses = call(
        back_sum_body,
        "back_sum",
        16 * 128 * 128,
        (shape((16, 128, 128), BF16), shape((1, 128), F32)),
        (),
        swap_all(pieces, "tensor"),
    )
    mine, other = call(
        grad_body,
        "grad_terms",
        6 * 128 * 2048 * 176,
        (shape((16, 192, 128), BF16),) * 2,
        (place,),
        losses,
        swap_all(blocks, "tensor"),
        hidden,
        preact,
        normed,
        down_weight.T,
    )
    pair = (mine.astype(F32) + lax.ppermute(other, "dp", CORES).astype(F32)).astype(BF16)
    pair = pair.reshape(4, 4, 192, 128)
    near = pair[0].astype(F32)
    for k, step in ((2, 2), (1, 1), (3, -1)):
        near += lax.ppermute(pair[k], "dp", ring_step(step)).astype(F32)
    near = near.astype(BF16)
    grad = shape((64, 176), F32)
    loss, grad_up, grad_down = call(
        finish_body,
        "finish",
        4 * 192 * 128,
        (shape((1, 1), F32), grad, grad),
        (jnp.reshape(loss_scale, (1,)),),
        swap_all(near, "dp", FAR),
    )
    return (jnp.reshape(loss, (1,)), grad_up, grad_down)


def solution(mesh):
    return jax.shard_map(
        on_device,
        mesh=mesh,
        in_specs=(
            P("dp", "tensor"),
            P("dp", "tensor"),
            P("tensor", "dp"),
            P("dp", None),
            P(),
            P("dp", None),
            P(None, "tensor"),
            P(None, "tensor"),
            P(None, "tensor"),
        ),
        out_specs=(P("dp"), P("dp", "tensor"), P("dp", "tensor")),
        check_vma=False,
    )
```

```python
import jax
import jax.numpy as jnp
from jax import lax
from jax.experimental import pallas as pl
from jax.experimental.pallas import tpu as pltpu
from jax.sharding import PartitionSpec as P

D = 8192
F32 = jnp.float32
BF16 = jnp.bfloat16

PLACES = [(zh, zl, c) for zh in range(4) for zl in range(4) for c in range(2)]
CORES = [(d, d ^ 1) for d in range(32)]
FAR = [[8 * h + 2 * l + c for h in range(4)] for l in range(4) for c in range(2)]
def index(zh, zl, c):
    return 8 * zh + 2 * zl + c


def ring_step(k):
    return [(d, (d + (2 - 4 * (d % 2)) * k) % 32) for d in range(32)]


FAR_STEP = [(index(zh, zl, c), index((zh - 1 + 2 * c) % 4, zl, c)) for zh, zl, c in PLACES]


NEAR = (0, 1, -1, 2)


def home_of(zh, zl, c, x, y):
    chip = (4 * zh + zl + NEAR[y] * (1 - 2 * c)) % 16
    return (2 * chip + c) * 16 + 4 * x + zl


HOME = [
    (index(zh, zl, c) * 16 + 4 * x + y, home_of(zh, zl, c, x, y))
    for zh, zl, c in PLACES
    for x in range(4)
    for y in range(4)
]


def swap_all(x, axis, groups=None):
    return lax.all_to_all(x, axis, split_axis=0, concat_axis=0, tiled=True, axis_index_groups=groups)


def call(body, name, flops, out_shape, scalars, *arrays):
    vmem = pl.BlockSpec(memory_space=pltpu.VMEM)
    smem = pl.BlockSpec(memory_space=pltpu.SMEM)
    return pl.pallas_call(
        body,
        out_shape=out_shape,
        in_specs=[smem] * len(scalars) + [vmem] * len(arrays),
        out_specs=jax.tree.map(lambda _: vmem, out_shape),
        compiler_params=pltpu.CompilerParams(vmem_limit_bytes=32 << 20),
        cost_estimate=pl.CostEstimate(flops=flops, bytes_accessed=2 << 20, transcendentals=0),
        name=name,
    )(*scalars, *arrays)


def halves(x):
    high = x.astype(BF16).astype(F32)
    return high, x - high


def both_body(own, other, out):
    out[0] = own[...]
    out[1] = other[...]


def forward_body(rows, up, down, normed, preact, hidden, pieces):
    x = rows[...].astype(F32)
    mean = jnp.mean(x * x, axis=-1, keepdims=True)
    normed[...] = (x * lax.rsqrt(mean + 1e-05)).astype(BF16)
    pre = lax.dot_general(normed[...], up[...], (((1,), (1,)), ((), ())), preferred_element_type=F32)
    preact[...] = pre
    units = (pre * jax.nn.sigmoid(pre)).astype(BF16)
    hidden[...] = units
    for pair in range(8):
        columns = slice(pair * 256, pair * 256 + 256)
        part = jnp.dot(units, down[:, columns], preferred_element_type=F32).astype(BF16)
        pieces[2 * pair] = part[:, :128]
        pieces[2 * pair + 1] = part[:, 128:]


def head_body(
    place_ref, student, mixed, own, near1, near2, near3, mine, pair, far, half, got, out
):
    zh, core, tensor = place_ref[0], place_ref[2], place_ref[4]
    mixed_sum = mixed[0].astype(F32)
    for t in range(1, 16):
        mixed_sum += mixed[t].astype(F32)
    block = student[:, pl.ds(pl.multiple_of(tensor * 128, 128), 128)].astype(F32)
    updated = (block + mixed_sum).astype(BF16)
    rows = jnp.concatenate([own[...], near1[...], near2[...], near3[...]], axis=0)

    def in_order(of_core, of_other):
        return jnp.where(core == 0, of_core, of_other), jnp.where(core == 0, of_other, of_core)

    def opposite(column_core):
        held = jnp.where(core == column_core, half[0], half[1])
        other = jnp.where(core == column_core, got[1, 256:], got[0, 256:])
        return jnp.concatenate(in_order(held, other), axis=0)

    side_step = jnp.where(core == 0, 1, 3)
    for step, sides in (
        (0, in_order(mine[...], pair[...])),
        (side_step, in_order(far[0], far[1])),
        (4 - side_step, in_order(got[1, :256], got[0, :256])),
        (2, (opposite(0), opposite(1))),
    ):
        for side, columns in enumerate(sides):
            part = jnp.dot(rows, columns, preferred_element_type=F32).astype(BF16)
            for near in range(4):
                piece = (zh + step) % 4 * 4 + near
                out[piece, :, side * 256 : side * 256 + 256] = part[near * 128 : near * 128 + 128]
    for t in range(16):
        out[t, :, 512:] = updated


def head_sum_body(got, head, updated):
    total = got[0, :, :512].astype(F32)
    for t in range(1, 16):
        total += got[t, :, :512].astype(F32)
    head[...] = total.astype(BF16)
    for t in range(16):
        updated[:, t * 128 : t * 128 + 128] = got[t, :, 512:]


def project_body(updated, proj, out):
    out[...] = jnp.dot(updated[...], proj[...], preferred_element_type=F32)


def residue_body(scale_ref, length_ref, owners, projected, resid, head, proj, pieces):
    scale, length = scale_ref[0], length_ref[0]
    target = (resid[...].astype(F32) + head[...].astype(F32)).astype(BF16)
    residue = projected[...] - target.astype(F32)
    row = lax.broadcasted_iota(jnp.int32, (128, 1), 0)
    live = (row < length).astype(F32)
    squares = live * jnp.sum(residue * residue, axis=-1, keepdims=True)
    owner = lax.broadcasted_iota(jnp.int32, (128, 128), 1)
    losses = jnp.sum(jnp.where(owners[...] == owner, squares, 0.0), axis=0, keepdims=True)
    high, low = halves(losses)
    side_row = lax.broadcasted_iota(jnp.int32, (16, 128), 0)
    side = jnp.where(side_row == 0, high, jnp.where(side_row == 1, low, 0.0)).astype(BF16)
    cotangent = (2.0 * scale * live * residue).astype(BF16)
    for pair in range(8):
        part = lax.dot_general(
            cotangent,
            proj[pair * 256 : pair * 256 + 256],
            (((1,), (1,)), ((), ())),
            preferred_element_type=F32,
        ).astype(BF16)
        pieces[2 * pair, :128] = part[:, :128]
        pieces[2 * pair + 1, :128] = part[:, 128:]
    for t in range(16):
        pieces[t, 128:] = side


def back_sum_body(got, out, losses):
    total = got[0].astype(F32)
    for t in range(1, 16):
        total += got[t].astype(F32)
    block = total[:128].astype(BF16)
    for t in range(16):
        out[t] = block
    losses[...] = total[128:129] + total[129:130]


def grad_body(place_ref, losses, blocks, hidden, preact, normed, down, mine, other):
    zl, core, source = place_ref[1], place_ref[2], place_ref[3]
    out_grad = jnp.concatenate([blocks[t] for t in range(16)], axis=1)
    hidden_grad = lax.dot_general(
        out_grad, down[...], (((1,), (1,)), ((), ())), preferred_element_type=F32
    )
    pre = preact[...]
    gate_sig = jax.nn.sigmoid(pre)
    pre_grad = hidden_grad * gate_sig * (1.0 + pre * (1.0 - gate_sig))
    up_left = pre_grad.T.astype(BF16)
    down_left = hidden[...].astype(F32).T.astype(BF16)
    lane = lax.broadcasted_iota(jnp.int32, (176, 128), 1)
    loss_lane = lax.broadcasted_iota(jnp.int32, (1, 128), 1)
    side_lane = lax.broadcasted_iota(jnp.int32, (16, 128), 1)
    for pair in range(8):
        columns = slice(pair * 256, pair * 256 + 256)
        up_pair = jnp.dot(up_left, normed[:, columns], preferred_element_type=F32)
        down_pair = jnp.dot(down_left, out_grad[:, columns], preferred_element_type=F32)
        for half in range(2):
            chip = 2 * pair + half
            ahead = (chip % 4 - zl + 4) % 4
            back = (4 - ahead) % 4
            own_piece = jnp.where(core == 0, ahead, back) * 4 + chip // 4
            other_piece = jnp.where(core == 0, back, ahead) * 4 + chip // 4
            up = up_pair[:, half * 128 : half * 128 + 128]
            below = down_pair[:, half * 128 : half * 128 + 128]
            even = jnp.where(lane < 64, up, pltpu.roll(below, 64, 1))
            odd = jnp.where(lane < 64, pltpu.roll(up, 64, 1), below)
            mine[own_piece, :176] = jnp.where(core == 0, even, odd).astype(BF16)
            other[other_piece, :176] = jnp.where(core == 0, odd, even).astype(BF16)
            for out, piece, owner in (
                (mine, own_piece, 2 * chip + core),
                (other, other_piece, 2 * chip + 1 - core),
            ):
                loss = jnp.where(loss_lane == owner, losses[...], 0.0)
                high, low = halves(jnp.sum(loss, axis=1, keepdims=True))
                side = jnp.where(
                    side_lane == 2 * source, high, jnp.where(side_lane == 2 * source + 1, low, 0.0)
                )
                out[piece, 176:] = side.astype(BF16)


def finish_body(scale_ref, got, loss, up, down):
    total = got[0].astype(F32)
    for zh in range(1, 4):
        total += got[zh].astype(F32)
    sums = jnp.sum(total[176:177], axis=1, keepdims=True)
    loss[...] = sums * scale_ref[0]
    grads = total[:176].T
    up[...] = grads[:64]
    down[...] = grads[64:]


def on_device(
    resid,
    context,
    out_weight,
    owners,
    query_lengths,
    student_rows,
    up_weight,
    down_weight,
    proj_weight,
):
    shape = jax.ShapeDtypeStruct
    dp = lax.axis_index("dp")
    place = jnp.stack([dp // 8, dp // 2 % 4, dp % 2, dp, lax.axis_index("tensor")]).astype(jnp.int32)
    loss_scale = 32.0 / (jnp.sum(query_lengths).astype(F32) * D)
    own_length = lax.dynamic_slice_in_dim(query_lengths, dp, 1)

    rows = [context] + [lax.ppermute(context, "dp", ring_step(-k)) for k in NEAR[1:]]
    pair = lax.ppermute(out_weight, "dp", CORES)
    both = call(both_body, "both_cores", 0, shape((2, 256, 256), BF16), (), out_weight, pair)
    far = lax.ppermute(both, "dp", FAR_STEP)

    normed, preact, hidden, mixed = call(
        forward_body,
        "forward",
        4 * 128 * 2048 * 176,
        (
            shape((128, 2048), BF16),
            shape((128, 176), F32),
            shape((128, 176), BF16),
            shape((16, 128, 128), BF16),
        ),
        (),
        student_rows,
        up_weight.T,
        down_weight.T,
    )
    rows, far, mixed = lax.optimization_barrier((rows, far, mixed))
    half = lax.dynamic_slice_in_dim(far, dp % 2 * 128, 128, axis=1)
    half = lax.ppermute(half, "dp", FAR_STEP)
    got = lax.ppermute(jnp.concatenate([far, half], axis=1), "dp", CORES)
    mixed = swap_all(mixed, "tensor")
    got, mixed = lax.optimization_barrier((got, mixed))
    parts = call(
        head_body,
        "head_parts",
        2 * 512 * 2048 * 256,
        shape((16, 128, 640), BF16),
        (place,),
        student_rows,
        mixed,
        *rows,
        out_weight,
        pair,
        far,
        half,
        got,
    )
    head, updated = call(
        head_sum_body,
        "head_sum",
        16 * 128 * 512,
        (shape((128, 512), BF16), shape((128, 2048), BF16)),
        (),
        swap_all(parts, "tensor"),
    )
    head = lax.ppermute(head, ("dp", "tensor"), HOME)
    projected = call(
        project_body, "project", 2 * 128 * 2048 * 512, shape((128, 512), F32), (), updated, proj_weight
    )
    pieces = call(
        residue_body,
        "residue",
        2 * 128 * 2048 * 512,
        shape((16, 144, 128), BF16),
        (jnp.reshape(loss_scale, (1,)), own_length),
        owners,
        projected,
        resid,
        head,
        proj_weight,
    )
    blocks, losses = call(
        back_sum_body,
        "back_sum",
        16 * 128 * 128,
        (shape((16, 128, 128), BF16), shape((1, 128), F32)),
        (),
        swap_all(pieces, "tensor"),
    )
    mine, other = call(
        grad_body,
        "grad_terms",
        6 * 128 * 2048 * 176,
        (shape((16, 192, 128), BF16),) * 2,
        (place,),
        losses,
        swap_all(blocks, "tensor"),
        hidden,
        preact,
        normed,
        down_weight.T,
    )
    pair = (mine.astype(F32) + lax.ppermute(other, "dp", CORES).astype(F32)).astype(BF16)
    pair = pair.reshape(4, 4, 192, 128)
    near = pair[0].astype(F32)
    for k, step in ((1, 1), (2, 2), (3, -1)):
        near += lax.ppermute(pair[k], "dp", ring_step(step)).astype(F32)
    near = near.astype(BF16)
    grad = shape((64, 176), F32)
    loss, grad_up, grad_down = call(
        finish_body,
        "finish",
        4 * 192 * 128,
        (shape((1, 1), F32), grad, grad),
        (jnp.reshape(loss_scale, (1,)),),
        swap_all(near, "dp", FAR),
    )
    return (jnp.reshape(loss, (1,)), grad_up, grad_down)


def solution(mesh):
    return jax.shard_map(
        on_device,
        mesh=mesh,
        in_specs=(
            P("dp", "tensor"),
            P("dp", "tensor"),
            P("tensor", "dp"),
            P("dp", None),
            P(),
            P("dp", None),
            P(None, "tensor"),
            P(None, "tensor"),
            P(None, "tensor"),
        ),
        out_specs=(P("dp"), P("dp", "tensor"), P("dp", "tensor")),
        check_vma=False,
    )
```

```python
import jax
import jax.numpy as jnp
from jax import lax
from jax.experimental import pallas as pl
from jax.experimental.pallas import tpu as pltpu
from jax.sharding import PartitionSpec as P

D = 8192
F32 = jnp.float32
BF16 = jnp.bfloat16

PLACES = [(zh, zl, c) for zh in range(4) for zl in range(4) for c in range(2)]
CORES = [(d, d ^ 1) for d in range(32)]
FAR = [
    [8 * (3 * c + (1 - 2 * c) * h) + 2 * l + c for h in range(4)] for l in range(4) for c in range(2)
]


def index(zh, zl, c):
    return 8 * zh + 2 * zl + c


def ring_step(k):
    return [(d, (d + (2 - 4 * (d % 2)) * k) % 32) for d in range(32)]


FAR_STEP = [(index(zh, zl, c), index((zh - 1 + 2 * c) % 4, zl, c)) for zh, zl, c in PLACES]


NEAR = (0, 1, -1, 2)


def home_of(zh, zl, c, x, y):
    chip = (4 * zh + zl + NEAR[y] * (1 - 2 * c)) % 16
    return (2 * chip + c) * 16 + 4 * x + zl


HOME = [
    (index(zh, zl, c) * 16 + 4 * x + y, home_of(zh, zl, c, x, y))
    for zh, zl, c in PLACES
    for x in range(4)
    for y in range(4)
]


def swap_all(x, axis, groups=None):
    return lax.all_to_all(x, axis, split_axis=0, concat_axis=0, tiled=True, axis_index_groups=groups)


def call(body, name, flops, out_shape, scalars, *arrays):
    vmem = pl.BlockSpec(memory_space=pltpu.VMEM)
    smem = pl.BlockSpec(memory_space=pltpu.SMEM)
    return pl.pallas_call(
        body,
        out_shape=out_shape,
        in_specs=[smem] * len(scalars) + [vmem] * len(arrays),
        out_specs=jax.tree.map(lambda _: vmem, out_shape),
        compiler_params=pltpu.CompilerParams(vmem_limit_bytes=32 << 20),
        cost_estimate=pl.CostEstimate(flops=flops, bytes_accessed=2 << 20, transcendentals=0),
        name=name,
    )(*scalars, *arrays)


def halves(x):
    high = x.astype(BF16).astype(F32)
    return high, x - high


def both_body(own, other, out):
    out[0] = own[...]
    out[1] = other[...]


def forward_body(rows, up, down, normed, preact, hidden, pieces):
    x = rows[...].astype(F32)
    mean = jnp.mean(x * x, axis=-1, keepdims=True)
    normed[...] = (x * lax.rsqrt(mean + 1e-05)).astype(BF16)
    pre = lax.dot_general(normed[...], up[...], (((1,), (1,)), ((), ())), preferred_element_type=F32)
    preact[...] = pre
    units = (pre * jax.nn.sigmoid(pre)).astype(BF16)
    hidden[...] = units
    for pair in range(8):
        columns = slice(pair * 256, pair * 256 + 256)
        part = jnp.dot(units, down[:, columns], preferred_element_type=F32).astype(BF16)
        pieces[2 * pair] = part[:, :128]
        pieces[2 * pair + 1] = part[:, 128:]


def head_body(
    place_ref, student, mixed, own, near1, near2, near3, mine, pair, far, half, got, out
):
    zh, core, tensor = place_ref[0], place_ref[2], place_ref[4]
    mixed_sum = mixed[0].astype(F32)
    for t in range(1, 16):
        mixed_sum += mixed[t].astype(F32)
    block = student[:, pl.ds(pl.multiple_of(tensor * 128, 128), 128)].astype(F32)
    updated = (block + mixed_sum).astype(BF16)
    rows = jnp.concatenate([own[...], near1[...], near2[...], near3[...]], axis=0)

    def in_order(of_core, of_other):
        return jnp.where(core == 0, of_core, of_other), jnp.where(core == 0, of_other, of_core)

    def opposite(column_core):
        held = jnp.where(core == column_core, half[0], half[1])
        other = jnp.where(core == column_core, got[1, 256:], got[0, 256:])
        return jnp.concatenate(in_order(held, other), axis=0)

    side_step = jnp.where(core == 0, 1, 3)
    for step, sides in (
        (0, in_order(mine[...], pair[...])),
        (side_step, in_order(far[0], far[1])),
        (4 - side_step, in_order(got[1, :256], got[0, :256])),
        (2, (opposite(0), opposite(1))),
    ):
        for side, columns in enumerate(sides):
            part = jnp.dot(rows, columns, preferred_element_type=F32).astype(BF16)
            for near in range(4):
                piece = (zh + step) % 4 * 4 + near
                out[piece, :, side * 256 : side * 256 + 256] = part[near * 128 : near * 128 + 128]
    for t in range(16):
        out[t, :, 512:] = updated


def head_sum_body(got, head, updated):
    total = got[0, :, :512].astype(F32)
    for t in range(1, 16):
        total += got[t, :, :512].astype(F32)
    head[...] = total.astype(BF16)
    for t in range(16):
        updated[:, t * 128 : t * 128 + 128] = got[t, :, 512:]


def project_body(updated, proj, out):
    out[...] = jnp.dot(updated[...], proj[...], preferred_element_type=F32)


def residue_body(scale_ref, length_ref, owners, projected, resid, head, proj, pieces):
    scale, length = scale_ref[0], length_ref[0]
    target = (resid[...].astype(F32) + head[...].astype(F32)).astype(BF16)
    residue = projected[...] - target.astype(F32)
    row = lax.broadcasted_iota(jnp.int32, (128, 1), 0)
    live = (row < length).astype(F32)
    squares = live * jnp.sum(residue * residue, axis=-1, keepdims=True)
    owner = lax.broadcasted_iota(jnp.int32, (128, 128), 1)
    losses = jnp.sum(jnp.where(owners[...] == owner, squares, 0.0), axis=0, keepdims=True)
    high, low = halves(losses)
    side_row = lax.broadcasted_iota(jnp.int32, (16, 128), 0)
    side = jnp.where(side_row == 0, high, jnp.where(side_row == 1, low, 0.0)).astype(BF16)
    cotangent = (2.0 * scale * live * residue).astype(BF16)
    for pair in range(8):
        part = lax.dot_general(
            cotangent,
            proj[pair * 256 : pair * 256 + 256],
            (((1,), (1,)), ((), ())),
            preferred_element_type=F32,
        ).astype(BF16)
        pieces[2 * pair, :128] = part[:, :128]
        pieces[2 * pair + 1, :128] = part[:, 128:]
    for t in range(16):
        pieces[t, 128:] = side


def back_sum_body(got, out, losses):
    total = got[0].astype(F32)
    for t in range(1, 16):
        total += got[t].astype(F32)
    block = total[:128].astype(BF16)
    for t in range(16):
        out[t] = block
    losses[...] = total[128:129] + total[129:130]


def grad_body(place_ref, losses, blocks, hidden, preact, normed, down, mine, other):
    zl, core, source = place_ref[1], place_ref[2], place_ref[3]
    out_grad = jnp.concatenate([blocks[t] for t in range(16)], axis=1)
    hidden_grad = lax.dot_general(
        out_grad, down[...], (((1,), (1,)), ((), ())), preferred_element_type=F32
    )
    pre = preact[...]
    gate_sig = jax.nn.sigmoid(pre)
    pre_grad = hidden_grad * gate_sig * (1.0 + pre * (1.0 - gate_sig))
    up_left = pre_grad.T.astype(BF16)
    down_left = hidden[...].astype(F32).T.astype(BF16)
    lane = lax.broadcasted_iota(jnp.int32, (176, 128), 1)
    loss_lane = lax.broadcasted_iota(jnp.int32, (1, 128), 1)
    side_lane = lax.broadcasted_iota(jnp.int32, (16, 128), 1)
    for pair in range(8):
        columns = slice(pair * 256, pair * 256 + 256)
        up_pair = jnp.dot(up_left, normed[:, columns], preferred_element_type=F32)
        down_pair = jnp.dot(down_left, out_grad[:, columns], preferred_element_type=F32)
        for half in range(2):
            chip = 2 * pair + half
            ahead = (chip % 4 - zl + 4) % 4
            back = (4 - ahead) % 4
            first, second = ahead * 4 + chip // 4, back * 4 + 3 - chip // 4
            own_piece = jnp.where(core == 0, first, second)
            other_piece = jnp.where(core == 0, second, first)
            up = up_pair[:, half * 128 : half * 128 + 128]
            below = down_pair[:, half * 128 : half * 128 + 128]
            even = jnp.where(lane < 64, up, pltpu.roll(below, 64, 1))
            odd = jnp.where(lane < 64, pltpu.roll(up, 64, 1), below)
            mine[own_piece, :176] = jnp.where(core == 0, even, odd).astype(BF16)
            other[other_piece, :176] = jnp.where(core == 0, odd, even).astype(BF16)
            for out, piece, owner in (
                (mine, own_piece, 2 * chip + core),
                (other, other_piece, 2 * chip + 1 - core),
            ):
                loss = jnp.where(loss_lane == owner, losses[...], 0.0)
                high, low = halves(jnp.sum(loss, axis=1, keepdims=True))
                side = jnp.where(
                    side_lane == 2 * source, high, jnp.where(side_lane == 2 * source + 1, low, 0.0)
                )
                out[piece, 176:] = side.astype(BF16)


def finish_body(scale_ref, got, loss, up, down):
    total = got[0].astype(F32)
    for zh in range(1, 4):
        total += got[zh].astype(F32)
    sums = jnp.sum(total[176:177], axis=1, keepdims=True)
    loss[...] = sums * scale_ref[0]
    grads = total[:176].T
    up[...] = grads[:64]
    down[...] = grads[64:]


def on_device(
    resid,
    context,
    out_weight,
    owners,
    query_lengths,
    student_rows,
    up_weight,
    down_weight,
    proj_weight,
):
    shape = jax.ShapeDtypeStruct
    dp = lax.axis_index("dp")
    place = jnp.stack([dp // 8, dp // 2 % 4, dp % 2, dp, lax.axis_index("tensor")]).astype(jnp.int32)
    loss_scale = 32.0 / (jnp.sum(query_lengths).astype(F32) * D)
    own_length = lax.dynamic_slice_in_dim(query_lengths, dp, 1)

    rows = [context] + [lax.ppermute(context, "dp", ring_step(-k)) for k in NEAR[1:]]
    pair = lax.ppermute(out_weight, "dp", CORES)
    both = call(both_body, "both_cores", 0, shape((2, 256, 256), BF16), (), out_weight, pair)
    far = lax.ppermute(both, "dp", FAR_STEP)

    normed, preact, hidden, mixed = call(
        forward_body,
        "forward",
        4 * 128 * 2048 * 176,
        (
            shape((128, 2048), BF16),
            shape((128, 176), F32),
            shape((128, 176), BF16),
            shape((16, 128, 128), BF16),
        ),
        (),
        student_rows,
        up_weight.T,
        down_weight.T,
    )
    rows, far, mixed = lax.optimization_barrier((rows, far, mixed))
    half = lax.dynamic_slice_in_dim(far, dp % 2 * 128, 128, axis=1)
    half = lax.ppermute(half, "dp", FAR_STEP)
    got = lax.ppermute(jnp.concatenate([far, half], axis=1), "dp", CORES)
    mixed = swap_all(mixed, "tensor")
    got, mixed = lax.optimization_barrier((got, mixed))
    parts = call(
        head_body,
        "head_parts",
        2 * 512 * 2048 * 256,
        shape((16, 128, 640), BF16),
        (place,),
        student_rows,
        mixed,
        *rows,
        out_weight,
        pair,
        far,
        half,
        got,
    )
    head, updated = call(
        head_sum_body,
        "head_sum",
        16 * 128 * 512,
        (shape((128, 512), BF16), shape((128, 2048), BF16)),
        (),
        swap_all(parts, "tensor"),
    )
    head = lax.ppermute(head, ("dp", "tensor"), HOME)
    projected = call(
        project_body, "project", 2 * 128 * 2048 * 512, shape((128, 512), F32), (), updated, proj_weight
    )
    pieces = call(
        residue_body,
        "residue",
        2 * 128 * 2048 * 512,
        shape((16, 144, 128), BF16),
        (jnp.reshape(loss_scale, (1,)), own_length),
        owners,
        projected,
        resid,
        head,
        proj_weight,
    )
    blocks, losses = call(
        back_sum_body,
        "back_sum",
        16 * 128 * 128,
        (shape((16, 128, 128), BF16), shape((1, 128), F32)),
        (),
        swap_all(pieces, "tensor"),
    )
    mine, other = call(
        grad_body,
        "grad_terms",
        6 * 128 * 2048 * 176,
        (shape((16, 192, 128), BF16),) * 2,
        (place,),
        losses,
        swap_all(blocks, "tensor"),
        hidden,
        preact,
        normed,
        down_weight.T,
    )
    pair = (mine.astype(F32) + lax.ppermute(other, "dp", CORES).astype(F32)).astype(BF16)
    pair = pair.reshape(4, 4, 192, 128)
    near = pair[0].astype(F32)
    for k, step in ((1, 1), (2, 2), (3, -1)):
        near += lax.ppermute(pair[k], "dp", ring_step(step)).astype(F32)
    near = near.astype(BF16)
    grad = shape((64, 176), F32)
    loss, grad_up, grad_down = call(
        finish_body,
        "finish",
        4 * 192 * 128,
        (shape((1, 1), F32), grad, grad),
        (jnp.reshape(loss_scale, (1,)),),
        swap_all(near, "dp", FAR),
    )
    return (jnp.reshape(loss, (1,)), grad_up, grad_down)


def solution(mesh):
    return jax.shard_map(
        on_device,
        mesh=mesh,
        in_specs=(
            P("dp", "tensor"),
            P("dp", "tensor"),
            P("tensor", "dp"),
            P("dp", None),
            P(),
            P("dp", None),
            P(None, "tensor"),
            P(None, "tensor"),
            P(None, "tensor"),
        ),
        out_specs=(P("dp"), P("dp", "tensor"), P("dp", "tensor")),
        check_vma=False,
    )
```

```python
import jax
import jax.numpy as jnp
from jax import lax
from jax.experimental import pallas as pl
from jax.experimental.pallas import tpu as pltpu
from jax.sharding import PartitionSpec as P

D = 8192
F32 = jnp.float32
BF16 = jnp.bfloat16

PLACES = [(zh, zl, c) for zh in range(4) for zl in range(4) for c in range(2)]
CORES = [(d, d ^ 1) for d in range(32)]
FAR = [
    [8 * (3 * c + (1 - 2 * c) * h) + 2 * l + c for h in range(4)] for l in range(4) for c in range(2)
]


def index(zh, zl, c):
    return 8 * zh + 2 * zl + c


def ring_step(k):
    return [(d, (d + (2 - 4 * (d % 2)) * k) % 32) for d in range(32)]


FAR_STEP = [(index(zh, zl, c), index((zh - 1 + 2 * c) % 4, zl, c)) for zh, zl, c in PLACES]


NEAR = (0, 1, -1, 2)


def home_of(zh, zl, c, x, y):
    chip = (4 * zh + zl + NEAR[y] * (1 - 2 * c)) % 16
    return (2 * chip + c) * 16 + 4 * x + zl


HOME = [
    (index(zh, zl, c) * 16 + 4 * x + y, home_of(zh, zl, c, x, y))
    for zh, zl, c in PLACES
    for x in range(4)
    for y in range(4)
]


ACROSS = [
    [d * 16 + (15 - t if d % 2 else t) for t in range(16)] for d in range(32)
]


def spot(core, t):
    return jnp.where(core == 0, t, 15 - t)


def across(x):
    return swap_all(x, ("dp", "tensor"), ACROSS)


def swap_all(x, axis, groups=None):
    return lax.all_to_all(x, axis, split_axis=0, concat_axis=0, tiled=True, axis_index_groups=groups)


def call(body, name, flops, out_shape, scalars, *arrays):
    vmem = pl.BlockSpec(memory_space=pltpu.VMEM)
    smem = pl.BlockSpec(memory_space=pltpu.SMEM)
    return pl.pallas_call(
        body,
        out_shape=out_shape,
        in_specs=[smem] * len(scalars) + [vmem] * len(arrays),
        out_specs=jax.tree.map(lambda _: vmem, out_shape),
        compiler_params=pltpu.CompilerParams(vmem_limit_bytes=32 << 20),
        cost_estimate=pl.CostEstimate(flops=flops, bytes_accessed=2 << 20, transcendentals=0),
        name=name,
    )(*scalars, *arrays)


def halves(x):
    high = x.astype(BF16).astype(F32)
    return high, x - high


def both_body(own, other, out):
    out[0] = own[...]
    out[1] = other[...]


def forward_body(place_ref, rows, up, down, normed, preact, hidden, pieces):
    x = rows[...].astype(F32)
    mean = jnp.mean(x * x, axis=-1, keepdims=True)
    normed[...] = (x * lax.rsqrt(mean + 1e-05)).astype(BF16)
    pre = lax.dot_general(normed[...], up[...], (((1,), (1,)), ((), ())), preferred_element_type=F32)
    preact[...] = pre
    units = (pre * jax.nn.sigmoid(pre)).astype(BF16)
    hidden[...] = units
    for pair in range(8):
        columns = slice(pair * 256, pair * 256 + 256)
        part = jnp.dot(units, down[:, columns], preferred_element_type=F32).astype(BF16)
        pieces[spot(place_ref[2], 2 * pair)] = part[:, :128]
        pieces[spot(place_ref[2], 2 * pair + 1)] = part[:, 128:]


def head_body(
    place_ref, student, mixed, own, near1, near2, near3, mine, pair, far, half, got, out
):
    zh, core, tensor = place_ref[0], place_ref[2], place_ref[4]
    mixed_sum = mixed[0].astype(F32)
    for t in range(1, 16):
        mixed_sum += mixed[t].astype(F32)
    block = student[:, pl.ds(pl.multiple_of(tensor * 128, 128), 128)].astype(F32)
    updated = (block + mixed_sum).astype(BF16)
    rows = jnp.concatenate([own[...], near1[...], near2[...], near3[...]], axis=0)

    def in_order(of_core, of_other):
        return jnp.where(core == 0, of_core, of_other), jnp.where(core == 0, of_other, of_core)

    def opposite(column_core):
        held = jnp.where(core == column_core, half[0], half[1])
        other = jnp.where(core == column_core, got[1, 256:], got[0, 256:])
        return jnp.concatenate(in_order(held, other), axis=0)

    side_step = jnp.where(core == 0, 1, 3)
    for step, sides in (
        (0, in_order(mine[...], pair[...])),
        (side_step, in_order(far[0], far[1])),
        (4 - side_step, in_order(got[1, :256], got[0, :256])),
        (2, (opposite(0), opposite(1))),
    ):
        for side, columns in enumerate(sides):
            part = jnp.dot(rows, columns, preferred_element_type=F32).astype(BF16)
            for near in range(4):
                piece = spot(core, (zh + step) % 4 * 4 + near)
                out[piece, :, side * 256 : side * 256 + 256] = part[near * 128 : near * 128 + 128]
    for t in range(16):
        out[t, :, 512:] = updated


def head_sum_body(place_ref, got, head, updated):
    total = got[0, :, :512].astype(F32)
    for t in range(1, 16):
        total += got[t, :, :512].astype(F32)
    head[...] = total.astype(BF16)
    for t in range(16):
        updated[:, t * 128 : t * 128 + 128] = got[spot(place_ref[2], t), :, 512:]


def project_body(updated, proj, out):
    out[...] = jnp.dot(updated[...], proj[...], preferred_element_type=F32)


def residue_body(place_ref, scale_ref, length_ref, owners, projected, resid, head, proj, pieces):
    scale, length = scale_ref[0], length_ref[0]
    target = (resid[...].astype(F32) + head[...].astype(F32)).astype(BF16)
    residue = projected[...] - target.astype(F32)
    row = lax.broadcasted_iota(jnp.int32, (128, 1), 0)
    live = (row < length).astype(F32)
    squares = live * jnp.sum(residue * residue, axis=-1, keepdims=True)
    owner = lax.broadcasted_iota(jnp.int32, (128, 128), 1)
    losses = jnp.sum(jnp.where(owners[...] == owner, squares, 0.0), axis=0, keepdims=True)
    high, low = halves(losses)
    side_row = lax.broadcasted_iota(jnp.int32, (16, 128), 0)
    side = jnp.where(side_row == 0, high, jnp.where(side_row == 1, low, 0.0)).astype(BF16)
    cotangent = (2.0 * scale * live * residue).astype(BF16)
    for pair in range(8):
        part = lax.dot_general(
            cotangent,
            proj[pair * 256 : pair * 256 + 256],
            (((1,), (1,)), ((), ())),
            preferred_element_type=F32,
        ).astype(BF16)
        pieces[spot(place_ref[2], 2 * pair), :128] = part[:, :128]
        pieces[spot(place_ref[2], 2 * pair + 1), :128] = part[:, 128:]
    for t in range(16):
        pieces[t, 128:] = side


def back_sum_body(got, out, losses):
    total = got[0].astype(F32)
    for t in range(1, 16):
        total += got[t].astype(F32)
    block = total[:128].astype(BF16)
    for t in range(16):
        out[t] = block
    losses[...] = total[128:129] + total[129:130]


def grad_body(place_ref, losses, blocks, hidden, preact, normed, down, mine, other):
    zl, core, source = place_ref[1], place_ref[2], place_ref[3]
    out_grad = jnp.concatenate([blocks[spot(core, t)] for t in range(16)], axis=1)
    hidden_grad = lax.dot_general(
        out_grad, down[...], (((1,), (1,)), ((), ())), preferred_element_type=F32
    )
    pre = preact[...]
    gate_sig = jax.nn.sigmoid(pre)
    pre_grad = hidden_grad * gate_sig * (1.0 + pre * (1.0 - gate_sig))
    up_left = pre_grad.T.astype(BF16)
    down_left = hidden[...].astype(F32).T.astype(BF16)
    lane = lax.broadcasted_iota(jnp.int32, (176, 128), 1)
    loss_lane = lax.broadcasted_iota(jnp.int32, (1, 128), 1)
    side_lane = lax.broadcasted_iota(jnp.int32, (16, 128), 1)
    for pair in range(8):
        columns = slice(pair * 256, pair * 256 + 256)
        up_pair = jnp.dot(up_left, normed[:, columns], preferred_element_type=F32)
        down_pair = jnp.dot(down_left, out_grad[:, columns], preferred_element_type=F32)
        for half in range(2):
            chip = 2 * pair + half
            ahead = (chip % 4 - zl + 4) % 4
            back = (4 - ahead) % 4
            first, second = ahead * 4 + chip // 4, back * 4 + 3 - chip // 4
            own_piece = jnp.where(core == 0, first, second)
            other_piece = jnp.where(core == 0, second, first)
            up = up_pair[:, half * 128 : half * 128 + 128]
            below = down_pair[:, half * 128 : half * 128 + 128]
            even = jnp.where(lane < 64, up, pltpu.roll(below, 64, 1))
            odd = jnp.where(lane < 64, pltpu.roll(up, 64, 1), below)
            mine[own_piece, :176] = jnp.where(core == 0, even, odd).astype(BF16)
            other[other_piece, :176] = jnp.where(core == 0, odd, even).astype(BF16)
            for out, piece, owner in (
                (mine, own_piece, 2 * chip + core),
                (other, other_piece, 2 * chip + 1 - core),
            ):
                loss = jnp.where(loss_lane == owner, losses[...], 0.0)
                high, low = halves(jnp.sum(loss, axis=1, keepdims=True))
                side = jnp.where(
                    side_lane == 2 * source, high, jnp.where(side_lane == 2 * source + 1, low, 0.0)
                )
                out[piece, 176:] = side.astype(BF16)


def finish_body(scale_ref, got, loss, up, down):
    total = got[0].astype(F32)
    for zh in range(1, 4):
        total += got[zh].astype(F32)
    sums = jnp.sum(total[176:177], axis=1, keepdims=True)
    loss[...] = sums * scale_ref[0]
    grads = total[:176].T
    up[...] = grads[:64]
    down[...] = grads[64:]


def on_device(
    resid,
    context,
    out_weight,
    owners,
    query_lengths,
    student_rows,
    up_weight,
    down_weight,
    proj_weight,
):
    shape = jax.ShapeDtypeStruct
    dp = lax.axis_index("dp")
    place = jnp.stack([dp // 8, dp // 2 % 4, dp % 2, dp, lax.axis_index("tensor")]).astype(jnp.int32)
    loss_scale = 32.0 / (jnp.sum(query_lengths).astype(F32) * D)
    own_length = lax.dynamic_slice_in_dim(query_lengths, dp, 1)

    rows = [context] + [lax.ppermute(context, "dp", ring_step(-k)) for k in NEAR[1:]]
    pair = lax.ppermute(out_weight, "dp", CORES)
    both = call(both_body, "both_cores", 0, shape((2, 256, 256), BF16), (), out_weight, pair)
    far = lax.ppermute(both, "dp", FAR_STEP)

    normed, preact, hidden, mixed = call(
        forward_body,
        "forward",
        4 * 128 * 2048 * 176,
        (
            shape((128, 2048), BF16),
            shape((128, 176), F32),
            shape((128, 176), BF16),
            shape((16, 128, 128), BF16),
        ),
        (place,),
        student_rows,
        up_weight.T,
        down_weight.T,
    )
    rows, far, mixed = lax.optimization_barrier((rows, far, mixed))
    half = lax.dynamic_slice_in_dim(far, dp % 2 * 128, 128, axis=1)
    half = lax.ppermute(half, "dp", FAR_STEP)
    got = lax.ppermute(jnp.concatenate([far, half], axis=1), "dp", CORES)
    mixed = across(mixed)
    got, mixed = lax.optimization_barrier((got, mixed))
    parts = call(
        head_body,
        "head_parts",
        2 * 512 * 2048 * 256,
        shape((16, 128, 640), BF16),
        (place,),
        student_rows,
        mixed,
        *rows,
        out_weight,
        pair,
        far,
        half,
        got,
    )
    head, updated = call(
        head_sum_body,
        "head_sum",
        16 * 128 * 512,
        (shape((128, 512), BF16), shape((128, 2048), BF16)),
        (place,),
        across(parts),
    )
    head = lax.ppermute(head, ("dp", "tensor"), HOME)
    projected = call(
        project_body, "project", 2 * 128 * 2048 * 512, shape((128, 512), F32), (), updated, proj_weight
    )
    pieces = call(
        residue_body,
        "residue",
        2 * 128 * 2048 * 512,
        shape((16, 144, 128), BF16),
        (place, jnp.reshape(loss_scale, (1,)), own_length),
        owners,
        projected,
        resid,
        head,
        proj_weight,
    )
    blocks, losses = call(
        back_sum_body,
        "back_sum",
        16 * 128 * 128,
        (shape((16, 128, 128), BF16), shape((1, 128), F32)),
        (),
        across(pieces),
    )
    mine, other = call(
        grad_body,
        "grad_terms",
        6 * 128 * 2048 * 176,
        (shape((16, 192, 128), BF16),) * 2,
        (place,),
        losses,
        across(blocks),
        hidden,
        preact,
        normed,
        down_weight.T,
    )
    pair = (mine.astype(F32) + lax.ppermute(other, "dp", CORES).astype(F32)).astype(BF16)
    pair = pair.reshape(4, 4, 192, 128)
    near = pair[0].astype(F32)
    for k, step in ((1, 1), (2, 2), (3, -1)):
        near += lax.ppermute(pair[k], "dp", ring_step(step)).astype(F32)
    near = near.astype(BF16)
    grad = shape((64, 176), F32)
    loss, grad_up, grad_down = call(
        finish_body,
        "finish",
        4 * 192 * 128,
        (shape((1, 1), F32), grad, grad),
        (jnp.reshape(loss_scale, (1,)),),
        swap_all(near, "dp", FAR),
    )
    return (jnp.reshape(loss, (1,)), grad_up, grad_down)


def solution(mesh):
    return jax.shard_map(
        on_device,
        mesh=mesh,
        in_specs=(
            P("dp", "tensor"),
            P("dp", "tensor"),
            P("tensor", "dp"),
            P("dp", None),
            P(),
            P("dp", None),
            P(None, "tensor"),
            P(None, "tensor"),
            P(None, "tensor"),
        ),
        out_specs=(P("dp"), P("dp", "tensor"), P("dp", "tensor")),
        check_vma=False,
    )
```
